256 devices in a mesh: dp: 64 (over z, x_hi, y), mp: 4 (over x_lo, core).
Axes of the slice: x: 4 (x_hi: 2, x_lo: 2; x = x_hi * 2 + x_lo), y: 4, z: 8, core: 2. Of those that a mesh axis runs over, the one named last changes fastest.
Arguments:
- teacher_in: bfloat16 [16384, 1024], P('dp'), may hold values from -6 to 6
- teacher_fc1: bfloat16 [1024, 4096], P(None, 'mp'), may hold values from -0.1875 to 0.1875
- teacher_fc2: bfloat16 [4096, 1024], P('mp'), may hold values from -0.09375 to 0.09375
- tok_in: bfloat16 [16384, 768], P('dp', 'mp'), may hold values from -6 to 6
- enc_proj: bfloat16 [768, 32], P('mp'), may hold values from -0.21875 to 0.21875
- codes: int32 [16384], P('dp'), may hold values from 0 to 8191
- ema_count: float32 [8192], replicated, may hold values from 0.5 to 8
- ema_sum: float32 [32, 8192], replicated, may hold values from -6 to 6
- dec_in: bfloat16 [32, 768], replicated, may hold values from -1 to 1
- head: bfloat16 [768, 1024], P(None, 'mp'), may hold values from -0.21875 to 0.21875
Outputs:
- new_count: float32 [8192], replicated
- new_sum: float32 [32, 8192], replicated
- grad_head: float32 [768, 1024], P(None, 'mp')
- grad_dec: float32 [32, 768], replicated
- grad_enc: float32 [768, 32], P('mp')
The draws below stay inside these ranges and needn't reach their ends.
All inputs are finite; a program needn't handle non-finite values.
Results may differ from the reference program's by a relative error of at most 0.015.
Values may be sent and summed in bfloat16 or wider, within the bound.
A program may use at most 64 MiB of HBM per device.

```python
import math
import jax
import jax.numpy as jnp
from jax import lax

DT = 1024
FT = 4096
DB = 768
CD = 32
CODES = 8192
ROWS = 16384
N_MP = 4


def touch_ends(result, rng, low, largest):
    spot = [jax.random.randint(jax.random.fold_in(rng, axis), (), 0, length) for axis, length in enumerate(result.shape)]
    main_axis = result.shape.index(max(result.shape))
    next_to = spot[:main_axis] + [(spot[main_axis] + 1) % result.shape[main_axis]] + spot[main_axis + 1:]
    return result.at[tuple(spot)].set(low).at[tuple(next_to)].set(largest)


def shard_levels(key, extent, split, low, largest):
    factor_of, own = 1.0, jax.random.fold_in(key, 6)
    for dim, parts in split:
        draws = jnp.exp(jax.random.uniform(jax.random.fold_in(own, dim), (parts,), jnp.float32, low / len(split), largest / len(split)))
        factor_of = factor_of * jnp.repeat(draws, extent[dim] // parts).reshape([-1 if axis == dim else 1 for axis in range(len(extent))])
    return factor_of


def centred(key, extent, scale, limit, shards=(), kind=jnp.bfloat16):
    result = jax.random.normal(key, extent, jnp.float32) * scale
    if len(shards) > 0:
        result = shard_levels(key, extent, shards, -0.22, 0.18) * result
    return jnp.clip(result, min=-limit, max=limit).astype(kind)


def setup_inputs(seed: int = 0) -> dict:
    keys = jax.random.split(jax.random.key(seed), 11)
    return {
        "teacher_in": centred(keys[0], (ROWS, DT), 1.0, 6.0, ((0, 64),)),
        "teacher_fc1": centred(keys[1], (DT, FT), DT ** -0.5, 0.1875, ((1, 4),)),
        "teacher_fc2": centred(keys[2], (FT, DT), FT ** -0.5, 0.09375, ((0, 4),)),
        "tok_in": centred(keys[3], (ROWS, DB), 1.0, 6.0, ((0, 64), (1, 4))),
        "enc_proj": centred(keys[4], (DB, CD), DB ** -0.5, 0.21875, ((0, 4),)),
        "codes": touch_ends(jax.random.randint(keys[5], (ROWS,), 0, CODES), jax.random.fold_in(keys[5], 1), 0, CODES - 1).astype(jnp.int32),
        "ema_count": jnp.clip(jnp.exp(jax.random.uniform(keys[6], (CODES,), jnp.float32, math.log(0.5), math.log(8.0))), 0.5, 8.0),
        "ema_sum": centred(keys[7], (CD, CODES), 1.0, 6.0, (), jnp.float32),
        "dec_in": centred(keys[8], (CD, DB), CD ** -0.5, 1.0),
        "head": centred(keys[9], (DB, DT), DB ** -0.5, 0.21875, ((1, 4),)),
    }


DECAY = 0.5
BETA = 0.25
EPS = 1e-06

def code_blocks(codes, z, codebook):
    total = codebook.shape[1]
    width = min(1024, total)
    blocks = total // width
    books = codebook.reshape(codebook.shape[0], blocks, width).transpose(1, 0, 2)

    def step(carry, inputs):
        block, book = inputs
        ids = block * width + jnp.arange(width, dtype=jnp.int32)
        onehot = (codes[:, None] == ids[None, :]).astype(jnp.float32)
        carry = carry + lax.dot_general(onehot, book, (((1,), (1,)), ((), ())), precision=lax.Precision.HIGHEST)
        sums = lax.dot_general(z, onehot, (((0,), (0,)), ((), ())), precision=lax.Precision.HIGHEST)
        return (carry, (lax.optimization_barrier(jnp.sum(onehot, axis=0)), sums))
    start = jnp.zeros((z.shape[0], codebook.shape[0]), jnp.float32)
    quant, (counts, sums) = lax.scan(step, start, (jnp.arange(blocks, dtype=jnp.int32), books))
    return (quant, counts.reshape(total), sums.transpose(1, 0, 2).reshape(codebook.shape[0], total))

def reference(teacher_in, teacher_fc1, teacher_fc2, tok_in, enc_proj, codes, ema_count, ema_sum, dec_in, head):
    teacher_hidden = jax.nn.gelu(jnp.dot(teacher_in, teacher_fc1, preferred_element_type=jnp.float32)).astype(jnp.bfloat16)
    share = FT // N_MP
    target = teacher_in.astype(jnp.float32)
    for group in range(N_MP):
        partial_value = jnp.dot(teacher_hidden[:, group * share:(group + 1) * share], teacher_fc2[group * share:(group + 1) * share], preferred_element_type=jnp.float32)
        target = target + lax.optimization_barrier(partial_value.astype(jnp.bfloat16)).astype(jnp.float32)
    z = jnp.dot(tok_in, enc_proj, preferred_element_type=jnp.float32)
    codebook = ema_sum / ema_count[None, :]
    quant, batch_count, batch_sum = code_blocks(codes, z, codebook)
    new_count = DECAY * ema_count + (1.0 - DECAY) * batch_count
    new_sum = DECAY * ema_sum + (1.0 - DECAY) * batch_sum
    q_round = quant.astype(jnp.bfloat16)
    pre = jnp.dot(q_round, dec_in, preferred_element_type=jnp.float32)
    hidden = jax.nn.gelu(pre).astype(jnp.bfloat16)
    pred = jnp.dot(hidden, head, preferred_element_type=jnp.float32)
    pp = lax.optimization_barrier(jnp.sum(pred * pred, axis=1))
    pt = lax.optimization_barrier(jnp.sum(pred * target, axis=1))
    tt = lax.optimization_barrier(jnp.sum(target * target, axis=1))
    norm_p = jnp.sqrt(pp + EPS)
    norm_t = jnp.sqrt(tt + EPS)
    dpred = (-target / (norm_p * norm_t)[:, None] + (pt / (norm_p ** 3 * norm_t))[:, None] * pred).astype(jnp.bfloat16)
    grad_head = lax.dot_general(hidden, dpred, (((0,), (0,)), ((), ())), preferred_element_type=jnp.float32)
    dh = lax.dot_general(dpred, head, (((1,), (1,)), ((), ())), preferred_element_type=jnp.float32)
    dpre = jax.vjp(jax.nn.gelu, pre)[1](dh)[0].astype(jnp.bfloat16)
    grad_dec = lax.dot_general(q_round, dpre, (((0,), (0,)), ((), ())), preferred_element_type=jnp.float32)
    dq = lax.dot_general(dpre, dec_in, (((1,), (1,)), ((), ())), preferred_element_type=jnp.float32)
    dz = (dq + 2.0 * BETA * (z - quant)).astype(jnp.bfloat16)
    grad_enc = lax.dot_general(tok_in, dz, (((0,), (0,)), ((), ())), preferred_element_type=jnp.float32)
    return (new_count, new_sum, grad_head, grad_dec, grad_enc)
```

```python
import functools
import math

import jax
import jax.numpy as jnp
from jax import lax
from jax.experimental import pallas as pl
from jax.experimental.pallas import tpu as pltpu
from jax.sharding import PartitionSpec as P

DECAY = 0.5
BETA = 0.25
EPS = 1e-06
MESH = pl.DeviceIdType.MESH
F32 = jnp.float32
BF16 = jnp.bfloat16
GELU_A = math.sqrt(2.0 / math.pi)
GELU_B = 0.044715

NMP = 4
GRP = 8
ZED = 8
ROWS = 256
OWN = 64
HI = 64
QHI = 16
SROW = 64
CROW = 16
GH = 96
GX = 16


def gelu(x):
    return 0.5 * x * (1.0 + jnp.tanh(GELU_A * (x + GELU_B * (x * x * x))))


def gelu_and_slope(x):
    square = x * x
    t = jnp.tanh(GELU_A * (x + GELU_B * (square * x)))
    value = 0.5 * x * (1.0 + t)
    slope = 0.5 * (1.0 + t) + (0.5 * GELU_A) * x * (1.0 - t * t) * (
        1.0 + (3.0 * GELU_B) * square
    )
    return value, slope


def dot(a, b, ca=1, cb=0):
    return lax.dot_general(a, b, (((ca,), (cb,)), ((), ())), preferred_element_type=F32)


def kernel(
    tin_h, fc1_h, fc2_h, tok_h, enc_h, codes_h, cnt_h, sum_h, dec_h, head_h,
    ncount_h, nsum_h, ghead_h, gdec_h, genc_h,
    tin, fc1, fc2, tok, enc, codes, cnt, inv, esum, dec,
    th, tp, hid_t, q_rows, book, pred,
    hd, tp_r, z_s, z_r, s_s, s_r, s_z, s_all, dp_s, dp_r, dpre, g_s, g_r, g_z, g_all,
    o_count, o_sum, o_head, o_dec, o_enc,
    load_sem, out_sem,
    hd_ss, hd_rs, tp_ss, tp_rs, z_ss, z_rs, s1_ss, s1_rs, s2_ss, s2_rs, s3_ss, s3_rs,
    s4_ss, s4_rs, dp_ss, dp_rs, dr_ss, dr_rs, g1_ss, g1_rs, x1_ss, x1_rs, g2_ss, g2_rs,
    g3_ss, g3_rs,
):
    dp = lax.axis_index("dp")
    mp = lax.axis_index("mp")
    zed = lax.div(dp, GRP)
    grp = lax.rem(dp, GRP)
    sib = mp + 1 - 2 * lax.rem(mp, 2)
    over = lax.rem(mp + 2, NMP)
    sib_over = lax.rem(sib + 2, NMP)

    def mp_peer(r):
        return (dp, lax.rem(mp + r, NMP))

    def grp_index(k):
        return lax.rem(grp + k, GRP)

    def grp_peer(k):
        return (zed * GRP + grp_index(k), mp)

    def zed_peer(k):
        return (lax.rem(zed + k, ZED) * GRP + grp, mp)

    wrap = (zed * GRP + grp_index(4), over)

    def remote(src, dst, ss, rs, dev):
        return pltpu.make_async_remote_copy(
            src_ref=src, dst_ref=dst, send_sem=ss, recv_sem=rs,
            device_id=dev, device_id_type=MESH,
        )

    barrier = pltpu.get_barrier_semaphore()
    peers = [mp_peer(r) for r in (1, 2, 3)] + [wrap]
    peers += [grp_peer(k) for k in range(1, GRP)] + [zed_peer(k) for k in range(1, ZED)]
    for dev in peers:
        pl.semaphore_signal(barrier, inc=1, device_id=dev, device_id_type=MESH)

    loads = []

    def load(src, dst):
        c = pltpu.make_async_copy(src, dst, load_sem.at[len(loads)])
        c.start()
        loads.append(c)
        return c

    l_tok = load(tok_h, tok)
    l_enc = load(enc_h, enc)
    l_tin = load(tin_h, tin)
    l_fc1 = [load(fc1_h.at[:, pl.ds(n * 256, 256)], fc1.at[n]) for n in range(4)]
    l_head = load(head_h, hd.at[mp])
    l_fc2 = [load(fc2_h.at[:, pl.ds(n * 256, 256)], fc2.at[n]) for n in range(4)]
    l_codes = load(codes_h, codes)
    l_cnt = load(cnt_h, cnt)
    l_sum = load(sum_h, esum)
    l_dec = load(dec_h, dec)

    l_tok.wait()
    l_enc.wait()
    z_part = dot(tok[...], enc[...])
    z_s[...] = z_part.T.astype(BF16)

    l_tin.wait()
    for n in range(4):
        l_fc1[n].wait()
        th[:, n * 256:(n + 1) * 256] = gelu(dot(tin[...], fc1[n])).astype(BF16)

    l_head.wait()
    pl.semaphore_wait(barrier, len(peers))

    c_z = [
        remote(z_s, z_r.at[r - 1], z_ss.at[r - 1], z_rs.at[r - 1], mp_peer(r)) for r in (1, 2, 3)
    ]
    for c in c_z:
        c.start()
    c_wrap = remote(hd.at[mp], hd.at[mp], hd_ss.at[0], hd_rs.at[0], wrap)
    c_wrap.start()
    c_sib = remote(hd.at[mp], hd.at[mp], hd_ss.at[1], hd_rs.at[1], (dp, sib))
    c_sib.start()

    c_tp = []
    for n in range(4):
        l_fc2[n].wait()
        tp[n] = dot(th[...], fc2[n]).astype(BF16)
        for r in (2, 1, 3):
            rows = pl.ds(pl.multiple_of(lax.rem(mp + r, NMP) * OWN, OWN), OWN)
            c = remote(
                tp.at[n, rows], tp_r.at[r - 1, n], tp_ss.at[n, r - 1], tp_rs.at[n, r - 1],
                mp_peer(r),
            )
            c.start()
            c_tp.append(c)

    l_codes.wait()
    l_cnt.wait()
    l_sum.wait()
    l_dec.wait()
    code = jnp.broadcast_to(codes[...], (32, ROWS))
    code_hi = jnp.right_shift(code, 7)
    code_lo = jnp.broadcast_to(jnp.bitwise_and(codes[...], 127), (128, ROWS))
    lo_id = lax.broadcasted_iota(jnp.int32, (128, ROWS), 0)
    lo_hot = jnp.where(lo_id == code_lo, 1.0, 0.0).astype(BF16)
    inv[...] = 1.0 / cnt[...]

    def look(i, total):
        for j in range(8):
            h = i * 8 + j
            part = esum[:, pl.ds(pl.multiple_of(h * 128, 128), 128)] * inv[pl.ds(h, 1), :]
            upper = part.astype(BF16)
            book[j * 32:(j + 1) * 32, 0:128] = upper
            book[j * 32:(j + 1) * 32, 128:256] = (part - upper.astype(F32)).astype(BF16)
        found = dot(book[...], jnp.concatenate([lo_hot, lo_hot], axis=0))
        for j in range(8):
            total = total + jnp.where(code_hi == i * 8 + j, found[j * 32:(j + 1) * 32], 0.0)
        return total

    q_t = lax.fori_loop(0, HI // 8, look, jnp.zeros((32, ROWS), F32))
    q_rows[...] = q_t.T
    q_round_t = q_t.astype(BF16)

    for c in c_z:
        c.wait()
    z_t = z_s[...].astype(F32)
    for r in range(3):
        z_t = z_t + z_r[r].astype(F32)
    z_upper = z_t.astype(BF16).astype(F32)
    z_lower = z_t - z_upper
    for i in range(QHI // 2):
        halves = []
        for part in (z_upper, z_lower):
            for j in range(2):
                halves.append(jnp.where(code_hi == mp * QHI + i * 2 + j, part, 0.0))
        both = dot(jnp.concatenate(halves, axis=0).astype(BF16), lo_hot, 1, 1)
        s_s[i, 0:SROW] = both[0:SROW] + both[SROW:2 * SROW]
    hi_id = lax.broadcasted_iota(jnp.int32, (CROW, ROWS), 0) + mp * QHI
    hi_hot = jnp.where(hi_id == code_hi[0:CROW], 1.0, 0.0).astype(BF16)
    counts = dot(hi_hot, lo_hot, 1, 1)
    for i in range(GRP):
        s_s[i, SROW:SROW + CROW] = counts
    c_s1 = []
    for k in (6, 2, 5, 7, 4, 1, 3):
        c = remote(
            s_s.at[grp_index(k)], s_r.at[k - 1], s1_ss.at[k - 1], s1_rs.at[k - 1], grp_peer(k)
        )
        c.start()
        c_s1.append(c)

    dec_t = dec[...].astype(F32).T.astype(BF16)
    for n in range(3):
        hid_t[n * 256:(n + 1) * 256, :] = gelu(
            dot(dec_t[n * 256:(n + 1) * 256], q_round_t)
        ).astype(BF16)
    own_rows = pl.ds(pl.multiple_of(mp * OWN, OWN), OWN)
    hidden, slope = gelu_and_slope(dot(q_rows[own_rows, :].astype(BF16), dec[...]))
    hidden = hidden.astype(BF16)

    c_wrap.wait()
    c_fwd = remote(hd.at[over], hd.at[over], hd_ss.at[2], hd_rs.at[2], (dp, sib))
    c_fwd.start()
    c_sib.wait()
    for b in (mp, sib, over):
        pred[b] = dot(hidden, hd[b])
    c_fwd.wait()
    pred[sib_over] = dot(hidden, hd[sib_over])

    for c in c_tp:
        c.wait()
    target = []
    for n in range(4):
        t = tin[own_rows, n * 256:(n + 1) * 256].astype(F32) + tp[n, own_rows, :].astype(F32)
        for r in range(3):
            t = t + tp_r[r, n].astype(F32)
        target.append(t)
    pp = jnp.zeros((OWN, 256), F32)
    pt = jnp.zeros((OWN, 256), F32)
    tt = jnp.zeros((OWN, 256), F32)
    for n in range(4):
        pp = pp + pred[n] * pred[n]
        pt = pt + pred[n] * target[n]
        tt = tt + target[n] * target[n]
    pp = jnp.sum(pp, axis=1, keepdims=True) + EPS
    pt = jnp.sum(pt, axis=1, keepdims=True)
    tt = jnp.sum(tt, axis=1, keepdims=True) + EPS
    inverse = 1.0 / (jnp.sqrt(pp) * jnp.sqrt(tt))
    scale = pt * inverse / pp
    for n in range(4):
        dp_s[n] = (scale * pred[n] - inverse * target[n]).astype(BF16)
    c_dp = []
    for r in (2, 1, 3):
        c = remote(
            dp_s.at[lax.rem(mp + r, NMP)], dp_r.at[mp], dp_ss.at[r - 1], dp_rs.at[r - 1],
            mp_peer(r),
        )
        c.start()
        c_dp.append(c)
    dp_r[mp] = dp_s[mp]
    dh = dot(dp_s[0], hd[0], 1, 1)
    for n in range(1, 4):
        dh = dh + dot(dp_s[n], hd[n], 1, 1)
    dpre[mp] = (dh * slope).astype(BF16)
    c_dr = []
    for r in (2, 1, 3):
        c = remote(dpre.at[mp], dpre.at[mp], dr_ss.at[r - 1], dr_rs.at[r - 1], mp_peer(r))
        c.start()
        c_dr.append(c)

    for c in c_s1:
        c.wait()
    s_part = s_s[grp]
    for k in range(GRP - 1):
        s_part = s_part + s_r[k]
    s_z[zed] = s_part
    c_s2 = []
    for k in (4, 3, 5, 2, 6, 1, 7):
        c = remote(s_z.at[zed], s_z.at[zed], s2_ss.at[k - 1], s2_rs.at[k - 1], zed_peer(k))
        c.start()
        c_s2.append(c)

    for c in c_dp:
        c.wait()
    grad = dot(hid_t[...], dp_r[...].reshape(ROWS, 256)).astype(BF16)
    for i in range(GRP):
        g_s[i, 0:GH] = grad[i * GH:(i + 1) * GH]
    c_g1 = []
    for k in (6, 2, 5, 7, 4, 1, 3):
        c = remote(
            g_s.at[grp_index(k), pl.ds(0, GH)], g_r.at[k - 1, pl.ds(0, GH)],
            g1_ss.at[k - 1], g1_rs.at[k - 1], grp_peer(k),
        )
        c.start()
        c_g1.append(c)

    for c in c_dr:
        c.wait()
    dpre_all = dpre[...].reshape(ROWS, 768)
    dq_t = dot(dec[...], dpre_all, 1, 1)
    dz_t = (dq_t + 2.0 * BETA * (z_t - q_t)).astype(BF16)
    grad_dec = dot(q_round_t, dpre_all).astype(BF16)
    grad_enc = dot(dz_t, tok[...]).astype(BF16)
    for n in range(3):
        for i in range(2):
            g_s[n * 2 + i, GH:GH + GX] = grad_dec[i * 16:(i + 1) * 16, n * 256:(n + 1) * 256]
    for i in range(2):
        g_s[6 + i, GH:GH + GX, 0:192] = grad_enc[i * 16:(i + 1) * 16]
        g_s[6 + i, GH:GH + GX, 192:256] = jnp.zeros((GX, 64), BF16)
    c_x1 = []
    for k in (6, 2, 5, 7, 4, 1, 3):
        c = remote(
            g_s.at[grp_index(k), pl.ds(GH, GX)], g_r.at[k - 1, pl.ds(GH, GX)],
            x1_ss.at[k - 1], x1_rs.at[k - 1], grp_peer(k),
        )
        c.start()
        c_x1.append(c)

    for c in c_s2:
        c.wait()
    s_part = s_z[0]
    for k in range(1, ZED):
        s_part = s_part + s_z[k]
    own_part = pl.ds(pl.multiple_of(grp * SROW, SROW), SROW)
    s_all[mp, own_part] = s_part[0:SROW]
    s_all[mp, pl.ds(GRP * SROW, CROW)] = s_part[SROW:SROW + CROW]
    c_s3 = []
    for k in (6, 2, 5, 7, 4, 1, 3):
        c = remote(
            s_all.at[mp, own_part], s_all.at[mp, own_part], s3_ss.at[k - 1], s3_rs.at[k - 1],
            grp_peer(k),
        )
        c.start()
        c_s3.append(c)

    for c in c_g1 + c_x1:
        c.wait()
    g_part = g_s[grp].astype(F32)
    for k in range(GRP - 1):
        g_part = g_part + g_r[k].astype(F32)
    g_z[zed] = g_part.astype(BF16)
    c_g2 = []
    for k in (4, 3, 5, 2, 6, 1, 7):
        c = remote(g_z.at[zed], g_z.at[zed], g2_ss.at[k - 1], g2_rs.at[k - 1], zed_peer(k))
        c.start()
        c_g2.append(c)

    for c in c_s3:
        c.wait()
    c_over = remote(s_all.at[mp], s_all.at[mp], s4_ss.at[0], s4_rs.at[0], (dp, over))
    c_over.start()
    c_near = remote(s_all.at[mp], s_all.at[mp], s4_ss.at[1], s4_rs.at[1], (dp, sib))
    c_near.start()
    c_over.wait()
    c_last = remote(s_all.at[over], s_all.at[over], s4_ss.at[2], s4_rs.at[2], (dp, sib))
    c_last.start()

    for c in c_g2:
        c.wait()
    g_part = g_z[0].astype(F32)
    for k in range(1, ZED):
        g_part = g_part + g_z[k].astype(F32)
    g_all[grp] = g_part.astype(BF16)
    c_g3 = []
    for k in (6, 2, 5, 7, 4, 1, 3):
        c = remote(g_all.at[grp], g_all.at[grp], g3_ss.at[k - 1], g3_rs.at[k - 1], grp_peer(k))
        c.start()
        c_g3.append(c)

    c_near.wait()
    c_last.wait()
    for m in range(NMP):
        o_count[m * CROW:(m + 1) * CROW] = s_all[m, GRP * SROW:GRP * SROW + CROW]
        for i in range(QHI):
            columns = slice((m * QHI + i) * 128, (m * QHI + i + 1) * 128)
            o_sum[:, columns] = DECAY * esum[:, columns] + (1.0 - DECAY) * s_all[
                m, i * 32:(i + 1) * 32
            ]
    o_count[...] = DECAY * cnt[...] + (1.0 - DECAY) * o_count[...]
    outs = []

    def store(src, dst):
        c = pltpu.make_async_copy(src, dst, out_sem.at[len(outs)])
        c.start()
        outs.append(c)

    store(o_count, ncount_h)
    store(o_sum, nsum_h)

    for c in c_g3:
        c.wait()
    for i in range(GRP):
        o_head[i * GH:(i + 1) * GH] = g_all[i, 0:GH].astype(F32)
    store(o_head, ghead_h)
    for n in range(3):
        for i in range(2):
            o_dec[i * 16:(i + 1) * 16, n * 256:(n + 1) * 256] = g_all[
                n * 2 + i, GH:GH + GX
            ].astype(F32)
    store(o_dec, gdec_h)
    enc_t = jnp.concatenate(
        [g_all[6, GH:GH + GX].astype(F32), g_all[7, GH:GH + GX].astype(F32)], axis=0
    )
    o_enc[...] = enc_t[:, 0:192].T
    store(o_enc, genc_h)
    for c in outs:
        c.wait()


def on_device(
    teacher_in, teacher_fc1, teacher_fc2, tok_in, enc_proj, codes, ema_count, ema_sum, dec_in, head
):
    def sems(*shape):
        return pltpu.SemaphoreType.DMA(shape)

    def two(*shape):
        return [sems(*shape), sems(*shape)]

    vm = pltpu.VMEM
    local = [
        vm((ROWS, 1024), BF16), vm((4, 1024, 256), BF16), vm((4, 1024, 256), BF16),
        vm((ROWS, 192), BF16), vm((192, 32), BF16), vm((1, ROWS), jnp.int32),
        vm((HI, 128), F32), vm((HI, 128), F32), vm((32, 8192), F32), vm((32, 768), BF16),
        vm((ROWS, 1024), BF16), vm((4, ROWS, 256), BF16), vm((768, ROWS), BF16),
        vm((ROWS, 32), F32), vm((256, 256), BF16), vm((4, OWN, 256), F32),
    ]
    exchanged = [
        vm((4, 768, 256), BF16), vm((3, 4, OWN, 256), BF16), vm((32, ROWS), BF16),
        vm((3, 32, ROWS), BF16),
        vm((GRP, SROW + CROW, 128), F32), vm((GRP - 1, SROW + CROW, 128), F32),
        vm((ZED, SROW + CROW, 128), F32), vm((NMP, GRP * SROW + CROW, 128), F32),
        vm((4, OWN, 256), BF16), vm((4, OWN, 256), BF16), vm((4, OWN, 768), BF16),
        vm((GRP, GH + GX, 256), BF16), vm((GRP - 1, GH + GX, 256), BF16),
        vm((ZED, GH + GX, 256), BF16), vm((GRP, GH + GX, 256), BF16),
    ]
    results = [
        vm((HI, 128), F32), vm((32, 8192), F32), vm((768, 256), F32), vm((32, 768), F32),
        vm((192, 32), F32),
    ]
    semaphores = [sems(17), sems(5)]
    semaphores += two(3) + two(4, 3) + two(3) + two(7) + two(7) + two(7)
    semaphores += two(3) + two(3) + two(3) + two(7) + two(7) + two(7) + two(7)
    anywhere = pl.BlockSpec(memory_space=pl.ANY)
    outs = pl.pallas_call(
        kernel,
        out_shape=(
            jax.ShapeDtypeStruct((HI, 128), F32),
            jax.ShapeDtypeStruct((32, 8192), F32),
            jax.ShapeDtypeStruct((768, 256), F32),
            jax.ShapeDtypeStruct((32, 768), F32),
            jax.ShapeDtypeStruct((192, 32), F32),
        ),
        in_specs=[anywhere] * 10,
        out_specs=(anywhere,) * 5,
        scratch_shapes=local + exchanged + results + semaphores,
        compiler_params=pltpu.CompilerParams(
            collective_id=0, has_side_effects=True, vmem_limit_bytes=40 * 2**20
        ),
        name="step",
    )(
        teacher_in, teacher_fc1, teacher_fc2, tok_in, enc_proj, codes.reshape(1, ROWS),
        ema_count.reshape(HI, 128), ema_sum, dec_in, head,
    )
    return (outs[0].reshape(8192), *outs[1:])


def solution(mesh):
    placed = (
        P("dp", None),
        P(None, "mp"),
        P("mp", None),
        P("dp", "mp"),
        P("mp", None),
        P("dp"),
        P(),
        P(),
        P(),
        P(None, "mp"),
    )
    return jax.shard_map(
        on_device,
        mesh=mesh,
        in_specs=placed,
        out_specs=(P(), P(), P(None, "mp"), P(), P("mp", None)),
        check_vma=False,
    )
```

```python
import functools
import math

import jax
import jax.numpy as jnp
from jax import lax
from jax.experimental import pallas as pl
from jax.experimental.pallas import tpu as pltpu
from jax.sharding import PartitionSpec as P

DECAY = 0.5
BETA = 0.25
EPS = 1e-06
MESH = pl.DeviceIdType.MESH
F32 = jnp.float32
BF16 = jnp.bfloat16
GELU_A = math.sqrt(2.0 / math.pi)
GELU_B = 0.044715

NMP = 4
GRP = 8
ZED = 8
ROWS = 256
OWN = 64
HI = 64
QHI = 16
SROW = 64
CROW = 16
GH = 96
GX = 16
GA = 48
FAR = (6, 2, 5, 7, 4, 1, 3)
FAR_Z = (4, 3, 5, 2, 6, 1, 7)


def gelu(x):
    return 0.5 * x * (1.0 + jnp.tanh(GELU_A * (x + GELU_B * (x * x * x))))


def gelu_and_slope(x):
    square = x * x
    t = jnp.tanh(GELU_A * (x + GELU_B * (square * x)))
    value = 0.5 * x * (1.0 + t)
    slope = 0.5 * (1.0 + t) + (0.5 * GELU_A) * x * (1.0 - t * t) * (
        1.0 + (3.0 * GELU_B) * square
    )
    return value, slope


def dot(a, b, ca=1, cb=0):
    return lax.dot_general(a, b, (((ca,), (cb,)), ((), ())), preferred_element_type=F32)


def kernel(
    tin_h, fc1_h, fc2_h, tok_h, enc_h, codes_h, cnt_h, sum_h, dec_h, head_h,
    ncount_h, nsum_h, ghead_h, gdec_h, genc_h,
    tin, fc1, fc2, tok, enc, codes, cnt, esum, dec,
    th, tp, hid_t, q_rows, book, pred,
    hd, tp_r, z_s, z_r, s_s, s_r, s_z, s_all, dp_s, dp_r, dpre, g_s, g_r, g_z, g_all,
    o_count, o_sum, o_head, o_dec, o_enc,
    load_sem, out_sem,
    hd_ss, hd_rs, tp_ss, tp_rs, z_ss, z_rs, s1_ss, s1_rs, s2_ss, s2_rs, s3_ss, s3_rs,
    s4_ss, s4_rs, dp_ss, dp_rs, dr_ss, dr_rs, g1_ss, g1_rs, x1_ss, x1_rs, g2_ss, g2_rs,
    g3_ss, g3_rs,
):
    dp = lax.axis_index("dp")
    mp = lax.axis_index("mp")
    zed = lax.div(dp, GRP)
    grp = lax.rem(dp, GRP)
    sib = mp + 1 - 2 * lax.rem(mp, 2)
    over = lax.rem(mp + 2, NMP)
    sib_over = lax.rem(sib + 2, NMP)

    def mp_peer(r):
        return (dp, lax.rem(mp + r, NMP))

    def grp_index(k):
        return lax.rem(grp + k, GRP)

    def grp_peer(k):
        return (zed * GRP + grp_index(k), mp)

    def zed_peer(k):
        return (lax.rem(zed + k, ZED) * GRP + grp, mp)

    wrap = (zed * GRP + grp_index(4), over)

    def remote(src, dst, ss, rs, dev):
        return pltpu.make_async_remote_copy(
            src_ref=src, dst_ref=dst, send_sem=ss, recv_sem=rs,
            device_id=dev, device_id_type=MESH,
        )

    barrier = pltpu.get_barrier_semaphore()
    peers = [mp_peer(r) for r in (1, 2, 3)] + [wrap]
    peers += [grp_peer(k) for k in range(1, GRP)] + [zed_peer(k) for k in range(1, ZED)]
    for dev in peers:
        pl.semaphore_signal(barrier, inc=1, device_id=dev, device_id_type=MESH)

    loads = []

    def load(src, dst):
        c = pltpu.make_async_copy(src, dst, load_sem.at[len(loads)])
        c.start()
        loads.append(c)
        return c

    l_tin = load(tin_h, tin)
    l_fc1 = [load(fc1_h.at[:, pl.ds(n * 256, 256)], fc1.at[n]) for n in range(4)]
    l_fc2 = [load(fc2_h.at[:, pl.ds(n * 256, 256)], fc2.at[n]) for n in range(4)]
    l_tok = load(tok_h, tok)
    l_enc = load(enc_h, enc)
    l_head = load(head_h, hd.at[mp])
    l_codes = load(codes_h, codes)
    l_cnt = load(cnt_h, cnt)
    l_sum = load(sum_h, esum)
    l_dec = load(dec_h, dec)

    l_tin.wait()
    for n in range(4):
        l_fc1[n].wait()
        th[:, n * 256:(n + 1) * 256] = gelu(dot(tin[...], fc1[n])).astype(BF16)
    for n in range(4):
        l_fc2[n].wait()
        tp[n] = dot(th[...], fc2[n]).astype(BF16)

    l_tok.wait()
    l_enc.wait()
    z_s[...] = dot(enc[...], tok[...]).astype(BF16)
    l_head.wait()

    pl.semaphore_wait(barrier, len(peers))
    c_z = [
        remote(z_s, z_r.at[r - 1], z_ss.at[r - 1], z_rs.at[r - 1], mp_peer(r)) for r in (2, 1, 3)
    ]
    for c in c_z:
        c.start()
    cuts = (pl.ds(0, 320), pl.ds(320, 320), pl.ds(640, 128))
    c_wrap = []
    for i, dev in enumerate((wrap, wrap, (dp, over))):
        c_wrap.append(
            remote(hd.at[mp, cuts[i]], hd.at[mp, cuts[i]], hd_ss.at[i], hd_rs.at[i], dev)
        )
    c_wrap[0].start()
    c_tp = []
    for r in (2, 1, 3):
        rows = pl.ds(pl.multiple_of(lax.rem(mp + r, NMP) * OWN, OWN), OWN)
        c = remote(
            tp.at[:, rows], tp_r.at[r - 1], tp_ss.at[r - 1], tp_rs.at[r - 1], mp_peer(r)
        )
        c.start()
        c_tp.append(c)
    c_wrap[1].start()
    c_wrap[2].start()
    c_sib = remote(hd.at[mp], hd.at[mp], hd_ss.at[3], hd_rs.at[3], (dp, sib))
    c_sib.start()

    l_codes.wait()
    l_cnt.wait()
    l_sum.wait()
    l_dec.wait()
    code = jnp.broadcast_to(codes[...], (32, ROWS))
    code_hi = jnp.right_shift(code, 7)
    code_lo = jnp.broadcast_to(jnp.bitwise_and(codes[...], 127), (128, ROWS))
    lo_id = lax.broadcasted_iota(jnp.int32, (128, ROWS), 0)
    lo_hot = jnp.where(lo_id == code_lo, 1.0, 0.0).astype(BF16)
    lo_twice = jnp.concatenate([lo_hot, lo_hot], axis=0)
    inv = 1.0 / cnt[...]
    for h in range(HI):
        part = esum[:, h * 128:(h + 1) * 128] * inv[h:h + 1, :]
        upper = part.astype(BF16)
        book[h * 32:(h + 1) * 32, 0:128] = upper
        book[h * 32:(h + 1) * 32, 128:256] = (part - upper.astype(F32)).astype(BF16)
    q_t = jnp.zeros((32, ROWS), F32)
    for i in range(HI // 8):
        found = dot(book[i * 256:(i + 1) * 256, :], lo_twice)
        for j in range(8):
            q_t = q_t + jnp.where(code_hi == i * 8 + j, found[j * 32:(j + 1) * 32], 0.0)
    q_rows[...] = q_t.T
    q_round_t = q_t.astype(BF16)
    own_rows = pl.ds(pl.multiple_of(mp * OWN, OWN), OWN)
    hidden, slope = gelu_and_slope(dot(q_rows[own_rows, :].astype(BF16), dec[...]))
    hidden = hidden.astype(BF16)

    for c in c_z:
        c.wait()
    z_t = z_s[...].astype(F32)
    for r in range(3):
        z_t = z_t + z_r[r].astype(F32)
    z_upper = z_t.astype(BF16).astype(F32)
    z_lower = z_t - z_upper
    for i in range(QHI // 2):
        halves = []
        for part in (z_upper, z_lower):
            for j in range(2):
                halves.append(jnp.where(code_hi == mp * QHI + i * 2 + j, part, 0.0))
        both = dot(jnp.concatenate(halves, axis=0).astype(BF16), lo_hot, 1, 1)
        s_s[i, 0:SROW] = both[0:SROW] + both[SROW:2 * SROW]
    hi_id = lax.broadcasted_iota(jnp.int32, (CROW, ROWS), 0) + mp * QHI
    hi_hot = jnp.where(hi_id == code_hi[0:CROW], 1.0, 0.0).astype(BF16)
    counts = dot(hi_hot, lo_hot, 1, 1)
    for i in range(GRP):
        s_s[i, SROW:SROW + CROW] = counts
    c_s1 = []
    for k in FAR:
        c = remote(
            s_s.at[grp_index(k)], s_r.at[k - 1], s1_ss.at[k - 1], s1_rs.at[k - 1], grp_peer(k)
        )
        c.start()
        c_s1.append(c)

    c_sib.wait()
    c_fwd = []
    for i in range(2):
        c_wrap[i].wait()
        c = remote(hd.at[over, cuts[i]], hd.at[over, cuts[i]], hd_ss.at[4 + i], hd_rs.at[4 + i], (dp, sib))
        c.start()
        c_fwd.append(c)
    c_wrap[2].wait()
    c = remote(hd.at[over, cuts[2]], hd.at[over, cuts[2]], hd_ss.at[6], hd_rs.at[6], (dp, sib))
    c.start()
    c_fwd.append(c)
    for b in (mp, sib, over):
        pred[b] = dot(hidden, hd[b])
    for c in c_fwd:
        c.wait()
    pred[sib_over] = dot(hidden, hd[sib_over])

    for c in c_tp:
        c.wait()
    target = []
    for n in range(4):
        t = tin[own_rows, n * 256:(n + 1) * 256].astype(F32) + tp[n, own_rows, :].astype(F32)
        for r in range(3):
            t = t + tp_r[r, n].astype(F32)
        target.append(t)
    pp = jnp.zeros((OWN, 256), F32)
    pt = jnp.zeros((OWN, 256), F32)
    tt = jnp.zeros((OWN, 256), F32)
    for n in range(4):
        pp = pp + pred[n] * pred[n]
        pt = pt + pred[n] * target[n]
        tt = tt + target[n] * target[n]
    pp = jnp.sum(pp, axis=1, keepdims=True) + EPS
    pt = jnp.sum(pt, axis=1, keepdims=True)
    tt = jnp.sum(tt, axis=1, keepdims=True) + EPS
    inverse = 1.0 / (jnp.sqrt(pp) * jnp.sqrt(tt))
    scale = pt * inverse / pp
    for n in range(4):
        dp_s[n] = (scale * pred[n] - inverse * target[n]).astype(BF16)
    c_dp = []
    for r in (2, 1, 3):
        c = remote(
            dp_s.at[lax.rem(mp + r, NMP)], dp_r.at[mp], dp_ss.at[r - 1], dp_rs.at[r - 1],
            mp_peer(r),
        )
        c.start()
        c_dp.append(c)
    dp_r[mp] = dp_s[mp]
    dh = dot(dp_s[0], hd[0], 1, 1)
    for n in range(1, 4):
        dh = dh + dot(dp_s[n], hd[n], 1, 1)
    dpre[mp] = (dh * slope).astype(BF16)
    c_dr = []
    for r in (2, 1, 3):
        c = remote(dpre.at[mp], dpre.at[mp], dr_ss.at[r - 1], dr_rs.at[r - 1], mp_peer(r))
        c.start()
        c_dr.append(c)

    dec_t = dec[...].astype(F32).T.astype(BF16)
    for n in range(3):
        hid_t[n * 256:(n + 1) * 256, :] = gelu(
            dot(dec_t[n * 256:(n + 1) * 256], q_round_t)
        ).astype(BF16)

    for c in c_dp:
        c.wait()
    grad = dot(hid_t[...], dp_r[...].reshape(ROWS, 256)).astype(BF16)
    for i in range(GRP):
        g_s[i, 0:GH] = grad[i * GH:(i + 1) * GH]
    c_g1 = [[], []]
    for part, rows in enumerate((pl.ds(0, GA), pl.ds(GA, GH - GA))):
        for k in FAR:
            c = remote(
                g_s.at[grp_index(k), rows], g_r.at[k - 1, rows],
                g1_ss.at[part, k - 1], g1_rs.at[part, k - 1], grp_peer(k),
            )
            c.start()
            c_g1[part].append(c)

    for c in c_s1:
        c.wait()
    s_part = s_s[grp]
    for k in range(GRP - 1):
        s_part = s_part + s_r[k]
    s_z[zed] = s_part
    c_s2 = []
    for k in FAR_Z:
        c = remote(s_z.at[zed], s_z.at[zed], s2_ss.at[k - 1], s2_rs.at[k - 1], zed_peer(k))
        c.start()
        c_s2.append(c)

    for c in c_dr:
        c.wait()
    dpre_all = dpre[...].reshape(ROWS, 768)
    dq_t = dot(dec[...], dpre_all, 1, 1)
    dz_t = (dq_t + 2.0 * BETA * (z_t - q_t)).astype(BF16)
    grad_dec = dot(q_round_t, dpre_all).astype(BF16)
    grad_enc = dot(dz_t, tok[...], 1, 1).astype(BF16)
    for n in range(3):
        for i in range(2):
            g_s[n * 2 + i, GH:GH + GX] = grad_dec[i * 16:(i + 1) * 16, n * 256:(n + 1) * 256]
    for i in range(2):
        g_s[6 + i, GH:GH + GX, 0:192] = grad_enc[i * 16:(i + 1) * 16]
        g_s[6 + i, GH:GH + GX, 192:256] = jnp.zeros((GX, 64), BF16)
    c_x1 = []
    for k in FAR:
        c = remote(
            g_s.at[grp_index(k), pl.ds(GH, GX)], g_r.at[k - 1, pl.ds(GH, GX)],
            x1_ss.at[k - 1], x1_rs.at[k - 1], grp_peer(k),
        )
        c.start()
        c_x1.append(c)

    halves = ((0, GA), (GA, GH + GX - GA))
    c_g2 = [[], []]
    for part, (first, size) in enumerate(halves):
        for c in c_g1[part] + (c_x1 if part == 1 else []):
            c.wait()
        g_part = g_s[grp, first:first + size].astype(F32)
        for k in range(GRP - 1):
            g_part = g_part + g_r[k, first:first + size].astype(F32)
        g_z[zed, first:first + size] = g_part.astype(BF16)
        for k in FAR_Z:
            rows = g_z.at[zed, pl.ds(first, size)]
            c = remote(rows, rows, g2_ss.at[part, k - 1], g2_rs.at[part, k - 1], zed_peer(k))
            c.start()
            c_g2[part].append(c)

    for c in c_s2:
        c.wait()
    s_part = s_z[0]
    for k in range(1, ZED):
        s_part = s_part + s_z[k]
    own_part = pl.ds(pl.multiple_of(grp * SROW, SROW), SROW)
    s_all[mp, own_part] = s_part[0:SROW]
    s_all[mp, pl.ds(GRP * SROW, CROW)] = s_part[SROW:SROW + CROW]
    c_s3 = []
    for k in FAR:
        c = remote(
            s_all.at[mp, own_part], s_all.at[mp, own_part], s3_ss.at[k - 1], s3_rs.at[k - 1],
            grp_peer(k),
        )
        c.start()
        c_s3.append(c)

    c_g3 = [[], []]
    for part, (first, size) in enumerate(halves):
        for c in c_g2[part]:
            c.wait()
        g_part = g_z[0, first:first + size].astype(F32)
        for k in range(1, ZED):
            g_part = g_part + g_z[k, first:first + size].astype(F32)
        g_all[grp, first:first + size] = g_part.astype(BF16)
        for k in FAR:
            rows = g_all.at[grp, pl.ds(first, size)]
            c = remote(rows, rows, g3_ss.at[part, k - 1], g3_rs.at[part, k - 1], grp_peer(k))
            c.start()
            c_g3[part].append(c)

    for c in c_s3:
        c.wait()
    c_over = remote(s_all.at[mp], s_all.at[mp], s4_ss.at[0], s4_rs.at[0], (dp, over))
    c_over.start()
    c_near = remote(s_all.at[mp], s_all.at[mp], s4_ss.at[1], s4_rs.at[1], (dp, sib))
    c_near.start()
    c_over.wait()
    c_last = remote(s_all.at[over], s_all.at[over], s4_ss.at[2], s4_rs.at[2], (dp, sib))
    c_last.start()

    c_near.wait()
    c_last.wait()
    outs = []

    def store(src, dst):
        c = pltpu.make_async_copy(src, dst, out_sem.at[len(outs)])
        c.start()
        outs.append(c)

    for m in range(NMP):
        o_count[m * CROW:(m + 1) * CROW] = (
            DECAY * cnt[m * CROW:(m + 1) * CROW]
            + (1.0 - DECAY) * s_all[m, GRP * SROW:GRP * SROW + CROW]
        )
        for i in range(QHI):
            columns = slice((m * QHI + i) * 128, (m * QHI + i + 1) * 128)
            o_sum[:, columns] = DECAY * esum[:, columns] + (1.0 - DECAY) * s_all[
                m, i * 32:(i + 1) * 32
            ]
    store(o_count, ncount_h)
    store(o_sum, nsum_h)

    for part, rows in enumerate((slice(0, GA), slice(GA, GH))):
        for c in c_g3[part]:
            c.wait()
        for i in range(GRP):
            o_head[i, rows] = g_all[i, rows].astype(F32)
        store(o_head.at[:, rows], ghead_h.at[:, rows])
    for n in range(3):
        for i in range(2):
            o_dec[i * 16:(i + 1) * 16, n * 256:(n + 1) * 256] = g_all[
                n * 2 + i, GH:GH + GX
            ].astype(F32)
    store(o_dec, gdec_h)
    for i in range(2):
        o_enc[i * 16:(i + 1) * 16] = g_all[6 + i, GH:GH + GX, 0:192].astype(F32)
    store(o_enc, genc_h)
    for c in outs:
        c.wait()


def copy_out(*refs):
    copies = [pltpu.make_async_copy(refs[i], refs[5 + i], refs[10].at[i]) for i in range(5)]
    for c in copies:
        c.start()
    for c in copies:
        c.wait()


def on_device(
    teacher_in, teacher_fc1, teacher_fc2, tok_in, enc_proj, codes, ema_count, ema_sum, dec_in, head
):
    def sems(*shape):
        return pltpu.SemaphoreType.DMA(shape)

    def two(*shape):
        return [sems(*shape), sems(*shape)]

    vm = pltpu.VMEM
    local = [
        vm((ROWS, 1024), BF16), vm((4, 1024, 256), BF16), vm((4, 1024, 256), BF16),
        vm((192, ROWS), BF16), vm((32, 192), BF16), vm((1, ROWS), jnp.int32),
        vm((HI, 128), F32), vm((32, 8192), F32), vm((32, 768), BF16),
        vm((ROWS, 1024), BF16), vm((4, ROWS, 256), BF16), vm((768, ROWS), BF16),
        vm((ROWS, 32), F32), vm((HI * 32, 256), BF16), vm((4, OWN, 256), F32),
    ]
    exchanged = [
        vm((4, 768, 256), BF16), vm((3, 4, OWN, 256), BF16), vm((32, ROWS), BF16),
        vm((3, 32, ROWS), BF16),
        vm((GRP, SROW + CROW, 128), F32), vm((GRP - 1, SROW + CROW, 128), F32),
        vm((ZED, SROW + CROW, 128), F32), vm((NMP, GRP * SROW + CROW, 128), F32),
        vm((4, OWN, 256), BF16), vm((4, OWN, 256), BF16), vm((4, OWN, 768), BF16),
        vm((GRP, GH + GX, 256), BF16), vm((GRP - 1, GH + GX, 256), BF16),
        vm((ZED, GH + GX, 256), BF16), vm((GRP, GH + GX, 256), BF16),
    ]
    results = [
        vm((HI, 128), F32), vm((32, 8192), F32), vm((GRP, GH, 256), F32), vm((32, 768), F32),
        vm((32, 192), F32),
    ]
    semaphores = [sems(16), sems(6)]
    semaphores += two(7) + two(3) + two(3) + two(7) + two(7) + two(7)
    semaphores += two(3) + two(3) + two(3) + two(2, 7) + two(7) + two(2, 7) + two(2, 7)
    anywhere = pl.BlockSpec(memory_space=pl.ANY)
    outs = pl.pallas_call(
        kernel,
        out_shape=(
            jax.ShapeDtypeStruct((HI, 128), F32),
            jax.ShapeDtypeStruct((32, 8192), F32),
            jax.ShapeDtypeStruct((GRP, GH, 256), F32),
            jax.ShapeDtypeStruct((32, 768), F32),
            jax.ShapeDtypeStruct((32, 192), F32),
        ),
        in_specs=[pl.BlockSpec(memory_space=pltpu.HBM)] * 10,
        out_specs=(anywhere,) * 5,
        scratch_shapes=local + exchanged + results + semaphores,
        compiler_params=pltpu.CompilerParams(
            collective_id=0, has_side_effects=True, vmem_limit_bytes=64 * 2**20
        ),
        name="step",
    )(
        teacher_in, teacher_fc1, teacher_fc2, tok_in.T, enc_proj.T, codes.reshape(1, ROWS),
        ema_count.reshape(HI, 128), ema_sum, dec_in, head,
    )
    outs = pl.pallas_call(
        copy_out,
        out_shape=tuple(jax.ShapeDtypeStruct(o.shape, o.dtype) for o in outs),
        in_specs=[anywhere] * 5,
        out_specs=(pl.BlockSpec(memory_space=pltpu.HBM),) * 5,
        scratch_shapes=[sems(5)],
        compiler_params=pltpu.CompilerParams(vmem_limit_bytes=64 * 2**20),
        name="results",
    )(*outs)
    return (outs[0].reshape(8192), outs[1], outs[2].reshape(768, 256), outs[3], outs[4].T)


def solution(mesh):
    placed = (
        P("dp", None),
        P(None, "mp"),
        P("mp", None),
        P("dp", "mp"),
        P("mp", None),
        P("dp"),
        P(),
        P(),
        P(),
        P(None, "mp"),
    )
    return jax.shard_map(
        on_device,
        mesh=mesh,
        in_specs=placed,
        out_specs=(P(), P(), P(None, "mp"), P(), P("mp", None)),
        check_vma=False,
    )
```

```python
import functools
import math

import jax
import jax.numpy as jnp
from jax import lax
from jax.experimental import pallas as pl
from jax.experimental.pallas import tpu as pltpu
from jax.sharding import PartitionSpec as P

DECAY = 0.5
BETA = 0.25
EPS = 1e-06
MESH = pl.DeviceIdType.MESH
F32 = jnp.float32
BF16 = jnp.bfloat16
GELU_A = math.sqrt(2.0 / math.pi)
GELU_B = 0.044715

NMP = 4
GRP = 8
ZED = 8
ROWS = 256
OWN = 64
HI = 64
QHI = 16
SROW = 64
CROW = 16
GH = 96
GX = 16
GA = 48
SPLIT = 264
FAR = (6, 2, 5, 7, 4, 1, 3)
FAR_Z = (4, 3, 5, 2, 6, 1, 7)


def gelu(x):
    return 0.5 * x * (1.0 + jnp.tanh(GELU_A * (x + GELU_B * (x * x * x))))


def gelu_and_slope(x):
    square = x * x
    t = jnp.tanh(GELU_A * (x + GELU_B * (square * x)))
    value = 0.5 * x * (1.0 + t)
    slope = 0.5 * (1.0 + t) + (0.5 * GELU_A) * x * (1.0 - t * t) * (
        1.0 + (3.0 * GELU_B) * square
    )
    return value, slope


def dot(a, b, ca=1, cb=0):
    return lax.dot_general(a, b, (((ca,), (cb,)), ((), ())), preferred_element_type=F32)


def kernel(
    tin_h, fc1_h, fc2_h, tok_h, enc_h, codes_h, cnt_h, sum_h, dec_h, head_h,
    ncount_h, nsum_h, ghead_h, gdec_h, genc_h,
    tin, fc1, fc2, tok, enc, codes, cnt, esum, dec,
    th, tp, hid_t, q_rows, book, pred,
    hd, tp_r, z_s, z_r, s_s, s_r, s_z, s_all, dp_s, dp_r, dpre, g_s, g_r, g_z, g_all,
    o_count, o_sum, o_head, o_dec, o_enc,
    load_sem, out_sem,
    hd_ss, hd_rs, tp_ss, tp_rs, z_ss, z_rs, s1_ss, s1_rs, s2_ss, s2_rs, s3_ss, s3_rs,
    s4_ss, s4_rs, dp_ss, dp_rs, dr_ss, dr_rs, g1_ss, g1_rs, x1_ss, x1_rs, g2_ss, g2_rs,
    g3_ss, g3_rs,
):
    dp = lax.axis_index("dp")
    mp = lax.axis_index("mp")
    zed = lax.div(dp, GRP)
    grp = lax.rem(dp, GRP)
    sib = mp + 1 - 2 * lax.rem(mp, 2)
    over = lax.rem(mp + 2, NMP)
    sib_over = lax.rem(sib + 2, NMP)

    def mp_peer(r):
        return (dp, lax.rem(mp + r, NMP))

    def grp_index(k):
        return lax.rem(grp + k, GRP)

    def grp_peer(k):
        return (zed * GRP + grp_index(k), mp)

    def zed_peer(k):
        return (lax.rem(zed + k, ZED) * GRP + grp, mp)

    wrap = (zed * GRP + grp_index(4), over)

    def remote(src, dst, ss, rs, dev):
        return pltpu.make_async_remote_copy(
            src_ref=src, dst_ref=dst, send_sem=ss, recv_sem=rs,
            device_id=dev, device_id_type=MESH,
        )

    barrier = pltpu.get_barrier_semaphore()
    peers = [mp_peer(r) for r in (1, 2, 3)] + [wrap]
    peers += [grp_peer(k) for k in range(1, GRP)] + [zed_peer(k) for k in range(1, ZED)]
    for dev in peers:
        pl.semaphore_signal(barrier, inc=1, device_id=dev, device_id_type=MESH)

    loads = []

    def load(src, dst):
        c = pltpu.make_async_copy(src, dst, load_sem.at[len(loads)])
        c.start()
        loads.append(c)
        return c

    l_tin = load(tin_h, tin)
    l_tok = load(tok_h, tok)
    l_enc = load(enc_h, enc)
    l_fc1 = [load(fc1_h.at[:, pl.ds(n * 256, 256)], fc1.at[n]) for n in range(4)]
    l_head = load(head_h, hd.at[mp])
    l_fc2 = [load(fc2_h.at[:, pl.ds(n * 256, 256)], fc2.at[n]) for n in range(4)]
    l_codes = load(codes_h, codes)
    l_cnt = load(cnt_h, cnt)
    l_sum = load(sum_h, esum)
    l_dec = load(dec_h, dec)

    l_tin.wait()
    for n in range(4):
        l_fc1[n].wait()
        th[:, n * 256:(n + 1) * 256] = gelu(dot(tin[...], fc1[n])).astype(BF16)

    l_tok.wait()
    l_enc.wait()
    z_s[...] = dot(enc[...], tok[...]).astype(BF16)
    l_head.wait()

    pl.semaphore_wait(barrier, len(peers))
    c_z = [
        remote(z_s, z_r.at[r - 1], z_ss.at[r - 1], z_rs.at[r - 1], mp_peer(r)) for r in (2, 1, 3)
    ]
    for c in c_z:
        c.start()
    cuts = (pl.ds(0, 320), pl.ds(320, 320), pl.ds(640, 128))
    c_wrap = []
    for i, dev in enumerate((wrap, wrap, (dp, over))):
        c_wrap.append(
            remote(hd.at[mp, cuts[i]], hd.at[mp, cuts[i]], hd_ss.at[i], hd_rs.at[i], dev)
        )
    for c in c_wrap:
        c.start()
    c_sib = remote(hd.at[mp], hd.at[mp], hd_ss.at[3], hd_rs.at[3], (dp, sib))
    c_sib.start()

    for n in range(4):
        l_fc2[n].wait()
        tp[n] = dot(th[...], fc2[n]).astype(BF16)
    c_tp = []
    for r in (2, 1, 3):
        rows = pl.ds(pl.multiple_of(lax.rem(mp + r, NMP) * OWN, OWN), OWN)
        c = remote(
            tp.at[:, rows], tp_r.at[r - 1], tp_ss.at[r - 1], tp_rs.at[r - 1], mp_peer(r)
        )
        c.start()
        c_tp.append(c)

    l_codes.wait()
    code = jnp.broadcast_to(codes[...], (32, ROWS))
    code_hi = jnp.right_shift(code, 7)
    code_lo = jnp.broadcast_to(jnp.bitwise_and(codes[...], 127), (128, ROWS))
    lo_id = lax.broadcasted_iota(jnp.int32, (128, ROWS), 0)
    lo_hot = jnp.where(lo_id == code_lo, 1.0, 0.0).astype(BF16)

    for c in c_z:
        c.wait()
    z_t = z_s[...].astype(F32)
    for r in range(3):
        z_t = z_t + z_r[r].astype(F32)
    z_upper = z_t.astype(BF16).astype(F32)
    z_lower = z_t - z_upper
    for i in range(QHI // 2):
        halves = []
        for part in (z_upper, z_lower):
            for j in range(2):
                halves.append(jnp.where(code_hi == mp * QHI + i * 2 + j, part, 0.0))
        both = dot(jnp.concatenate(halves, axis=0).astype(BF16), lo_hot, 1, 1)
        s_s[i, 0:SROW] = both[0:SROW] + both[SROW:2 * SROW]
    hi_id = lax.broadcasted_iota(jnp.int32, (CROW, ROWS), 0) + mp * QHI
    hi_hot = jnp.where(hi_id == code_hi[0:CROW], 1.0, 0.0).astype(BF16)
    counts = dot(hi_hot, lo_hot, 1, 1)
    for i in range(GRP):
        s_s[i, SROW:SROW + CROW] = counts
    c_s1 = []
    for k in FAR:
        c = remote(
            s_s.at[grp_index(k)], s_r.at[k - 1], s1_ss.at[k - 1], s1_rs.at[k - 1], grp_peer(k)
        )
        c.start()
        c_s1.append(c)

    l_cnt.wait()
    l_sum.wait()
    l_dec.wait()
    lo_twice = jnp.concatenate([lo_hot, lo_hot], axis=0)
    inv = 1.0 / cnt[...]
    for h in range(HI):
        part = esum[:, h * 128:(h + 1) * 128] * inv[h:h + 1, :]
        upper = part.astype(BF16)
        book[h * 32:(h + 1) * 32, 0:128] = upper
        book[h * 32:(h + 1) * 32, 128:256] = (part - upper.astype(F32)).astype(BF16)
    q_t = jnp.zeros((32, ROWS), F32)
    for i in range(HI // 8):
        found = dot(book[i * 256:(i + 1) * 256, :], lo_twice)
        for j in range(8):
            q_t = q_t + jnp.where(code_hi == i * 8 + j, found[j * 32:(j + 1) * 32], 0.0)
    q_rows[...] = q_t.T
    q_round_t = q_t.astype(BF16)
    own_rows = pl.ds(pl.multiple_of(mp * OWN, OWN), OWN)
    hidden, slope = gelu_and_slope(dot(q_rows[own_rows, :].astype(BF16), dec[...]))
    hidden = hidden.astype(BF16)

    c_sib.wait()
    c_fwd = []
    for i in range(3):
        c_wrap[i].wait()
        rows = hd.at[over, cuts[i]]
        c = remote(rows, rows, hd_ss.at[4 + i], hd_rs.at[4 + i], (dp, sib))
        c.start()
        c_fwd.append(c)
    for b in (mp, sib, over):
        pred[b] = dot(hidden, hd[b])
    for c in c_fwd:
        c.wait()
    pred[sib_over] = dot(hidden, hd[sib_over])

    for c in c_tp:
        c.wait()
    target = []
    for n in range(4):
        t = tin[own_rows, n * 256:(n + 1) * 256].astype(F32) + tp[n, own_rows, :].astype(F32)
        for r in range(3):
            t = t + tp_r[r, n].astype(F32)
        target.append(t)
    pp = jnp.zeros((OWN, 256), F32)
    pt = jnp.zeros((OWN, 256), F32)
    tt = jnp.zeros((OWN, 256), F32)
    for n in range(4):
        pp = pp + pred[n] * pred[n]
        pt = pt + pred[n] * target[n]
        tt = tt + target[n] * target[n]
    pp = jnp.sum(pp, axis=1, keepdims=True) + EPS
    pt = jnp.sum(pt, axis=1, keepdims=True)
    tt = jnp.sum(tt, axis=1, keepdims=True) + EPS
    inverse = 1.0 / (jnp.sqrt(pp) * jnp.sqrt(tt))
    scale = pt * inverse / pp
    for n in range(4):
        dp_s[n] = (scale * pred[n] - inverse * target[n]).astype(BF16)
    c_dp = []
    for r in (2, 1, 3):
        c = remote(
            dp_s.at[lax.rem(mp + r, NMP)], dp_r.at[mp], dp_ss.at[r - 1], dp_rs.at[r - 1],
            mp_peer(r),
        )
        c.start()
        c_dp.append(c)
    dp_r[mp] = dp_s[mp]
    dh = dot(dp_s[0], hd[0], 1, 1)
    for n in range(1, 4):
        dh = dh + dot(dp_s[n], hd[n], 1, 1)
    dpre[mp] = (dh * slope).astype(BF16)
    c_dr = []
    for r in (2, 1, 3):
        c = remote(dpre.at[mp], dpre.at[mp], dr_ss.at[r - 1], dr_rs.at[r - 1], mp_peer(r))
        c.start()
        c_dr.append(c)

    for c in c_s1:
        c.wait()
    s_part = s_s[grp]
    for k in range(GRP - 1):
        s_part = s_part + s_r[k]
    s_z[zed] = s_part
    c_s2 = []
    for k in FAR_Z:
        c = remote(s_z.at[zed], s_z.at[zed], s2_ss.at[k - 1], s2_rs.at[k - 1], zed_peer(k))
        c.start()
        c_s2.append(c)

    dec_t = dec[...].astype(F32).T.astype(BF16)
    for n in range(3):
        hid_t[n * 256:(n + 1) * 256, :] = gelu(
            dot(dec_t[n * 256:(n + 1) * 256], q_round_t)
        ).astype(BF16)

    for c in c_dp:
        c.wait()
    grad = dot(hid_t[...], dp_r[...].reshape(ROWS, 256)).astype(BF16)
    for i in range(GRP):
        g_s[i, 0:GH] = grad[i * GH:(i + 1) * GH]
    c_g1 = [[], []]
    for part, rows in enumerate((pl.ds(0, GA), pl.ds(GA, GH - GA))):
        for k in FAR:
            c = remote(
                g_s.at[grp_index(k), rows], g_r.at[k - 1, rows],
                g1_ss.at[part, k - 1], g1_rs.at[part, k - 1], grp_peer(k),
            )
            c.start()
            c_g1[part].append(c)

    for c in c_dr:
        c.wait()
    dpre_all = dpre[...].reshape(ROWS, 768)
    dq_t = dot(dec[...], dpre_all, 1, 1)
    dz_t = (dq_t + 2.0 * BETA * (z_t - q_t)).astype(BF16)
    grad_dec = dot(q_round_t, dpre_all).astype(BF16)
    grad_enc = dot(dz_t, tok[...], 1, 1).astype(BF16)
    for n in range(3):
        for i in range(2):
            g_s[n * 2 + i, GH:GH + GX] = grad_dec[i * 16:(i + 1) * 16, n * 256:(n + 1) * 256]
    for i in range(2):
        g_s[6 + i, GH:GH + GX, 0:192] = grad_enc[i * 16:(i + 1) * 16]
        g_s[6 + i, GH:GH + GX, 192:256] = jnp.zeros((GX, 64), BF16)
    c_x1 = []
    for k in FAR:
        c = remote(
            g_s.at[grp_index(k), pl.ds(GH, GX)], g_r.at[k - 1, pl.ds(GH, GX)],
            x1_ss.at[k - 1], x1_rs.at[k - 1], grp_peer(k),
        )
        c.start()
        c_x1.append(c)

    halves = ((0, GA), (GA, GH + GX - GA))
    c_g2 = [[], []]
    c_g3 = [[], []]

    def along_z(part):
        first, size = halves[part]
        g_part = g_s[grp, first:first + size].astype(F32)
        for k in range(GRP - 1):
            g_part = g_part + g_r[k, first:first + size].astype(F32)
        g_z[zed, first:first + size] = g_part.astype(BF16)
        for k in FAR_Z:
            rows = g_z.at[zed, pl.ds(first, size)]
            c = remote(rows, rows, g2_ss.at[part, k - 1], g2_rs.at[part, k - 1], zed_peer(k))
            c.start()
            c_g2[part].append(c)

    def gather(part):
        first, size = halves[part]
        for c in c_g2[part]:
            c.wait()
        g_part = g_z[0, first:first + size].astype(F32)
        for k in range(1, ZED):
            g_part = g_part + g_z[k, first:first + size].astype(F32)
        g_all[grp, first:first + size] = g_part.astype(BF16)
        for k in FAR:
            rows = g_all.at[grp, pl.ds(first, size)]
            c = remote(rows, rows, g3_ss.at[part, k - 1], g3_rs.at[part, k - 1], grp_peer(k))
            c.start()
            c_g3[part].append(c)

    for c in c_g1[0]:
        c.wait()
    along_z(0)

    for c in c_s2:
        c.wait()
    s_part = s_z[0]
    for k in range(1, ZED):
        s_part = s_part + s_z[k]
    own_part = pl.ds(pl.multiple_of(grp * SROW, SROW), SROW)
    s_all[mp, own_part] = s_part[0:SROW]
    s_all[mp, pl.ds(GRP * SROW, CROW)] = s_part[SROW:SROW + CROW]
    c_s3 = []
    for k in FAR:
        c = remote(
            s_all.at[mp, own_part], s_all.at[mp, own_part], s3_ss.at[k - 1], s3_rs.at[k - 1],
            grp_peer(k),
        )
        c.start()
        c_s3.append(c)

    for c in c_g1[1] + c_x1:
        c.wait()
    along_z(1)
    gather(0)

    for c in c_s3:
        c.wait()
    parts = (pl.ds(0, SPLIT), pl.ds(SPLIT, GRP * SROW + CROW - SPLIT))
    c_over = []
    for i, dev in enumerate(((dp, over), wrap)):
        rows = s_all.at[mp, parts[i]]
        c = remote(rows, rows, s4_ss.at[i], s4_rs.at[i], dev)
        c.start()
        c_over.append(c)
    c_near = remote(s_all.at[mp], s_all.at[mp], s4_ss.at[2], s4_rs.at[2], (dp, sib))
    c_near.start()

    gather(1)
    c_last = []
    for i in range(2):
        c_over[i].wait()
        rows = s_all.at[over, parts[i]]
        c = remote(rows, rows, s4_ss.at[3 + i], s4_rs.at[3 + i], (dp, sib))
        c.start()
        c_last.append(c)

    for c in c_last + [c_near]:
        c.wait()
    outs = []

    def store(src, dst):
        c = pltpu.make_async_copy(src, dst, out_sem.at[len(outs)])
        c.start()
        outs.append(c)

    for m in range(NMP):
        o_count[m * CROW:(m + 1) * CROW] = (
            DECAY * cnt[m * CROW:(m + 1) * CROW]
            + (1.0 - DECAY) * s_all[m, GRP * SROW:GRP * SROW + CROW]
        )
        for i in range(QHI):
            columns = slice((m * QHI + i) * 128, (m * QHI + i + 1) * 128)
            o_sum[:, columns] = DECAY * esum[:, columns] + (1.0 - DECAY) * s_all[
                m, i * 32:(i + 1) * 32
            ]
    store(o_count, ncount_h)
    store(o_sum, nsum_h)

    for part, rows in enumerate((slice(0, GA), slice(GA, GH))):
        for c in c_g3[part]:
            c.wait()
        for i in range(GRP):
            o_head[i, rows] = g_all[i, rows].astype(F32)
        store(o_head.at[:, rows], ghead_h.at[:, rows])
    for n in range(3):
        for i in range(2):
            o_dec[i * 16:(i + 1) * 16, n * 256:(n + 1) * 256] = g_all[
                n * 2 + i, GH:GH + GX
            ].astype(F32)
    store(o_dec, gdec_h)
    for i in range(2):
        o_enc[i * 16:(i + 1) * 16] = g_all[6 + i, GH:GH + GX, 0:192].astype(F32)
    store(o_enc, genc_h)
    for c in outs:
        c.wait()


def copy_out(*refs):
    arrays, results, buffers, (in_sem, out_sem) = refs[0:5], refs[5:10], refs[10:15], refs[15:]
    pieces = [(1, (slice(None), pl.ds(i * 2048, 2048))) for i in range(4)]
    pieces += [(2, (pl.ds(i * 2, 2),)) for i in range(4)]
    pieces += [(i, (slice(None),)) for i in (0, 3, 4)]
    ins = []
    for i, (a, at) in enumerate(pieces):
        c = pltpu.make_async_copy(arrays[a].at[at], buffers[a].at[at], in_sem.at[i])
        c.start()
        ins.append(c)
    outs = []
    for i, (a, at) in enumerate(pieces):
        ins[i].wait()
        c = pltpu.make_async_copy(buffers[a].at[at], results[a].at[at], out_sem.at[i])
        c.start()
        outs.append(c)
    for c in outs:
        c.wait()


def on_device(
    teacher_in, teacher_fc1, teacher_fc2, tok_in, enc_proj, codes, ema_count, ema_sum, dec_in, head
):
    def sems(*shape):
        return pltpu.SemaphoreType.DMA(shape)

    def two(*shape):
        return [sems(*shape), sems(*shape)]

    vm = pltpu.VMEM
    local = [
        vm((ROWS, 1024), BF16), vm((4, 1024, 256), BF16), vm((4, 1024, 256), BF16),
        vm((192, ROWS), BF16), vm((32, 192), BF16), vm((1, ROWS), jnp.int32),
        vm((HI, 128), F32), vm((32, 8192), F32), vm((32, 768), BF16),
        vm((ROWS, 1024), BF16), vm((4, ROWS, 256), BF16), vm((768, ROWS), BF16),
        vm((ROWS, 32), F32), vm((HI * 32, 256), BF16), vm((4, OWN, 256), F32),
    ]
    exchanged = [
        vm((4, 768, 256), BF16), vm((3, 4, OWN, 256), BF16), vm((32, ROWS), BF16),
        vm((3, 32, ROWS), BF16),
        vm((GRP, SROW + CROW, 128), F32), vm((GRP - 1, SROW + CROW, 128), F32),
        vm((ZED, SROW + CROW, 128), F32), vm((NMP, GRP * SROW + CROW, 128), F32),
        vm((4, OWN, 256), BF16), vm((4, OWN, 256), BF16), vm((4, OWN, 768), BF16),
        vm((GRP, GH + GX, 256), BF16), vm((GRP - 1, GH + GX, 256), BF16),
        vm((ZED, GH + GX, 256), BF16), vm((GRP, GH + GX, 256), BF16),
    ]
    results = [
        vm((HI, 128), F32), vm((32, 8192), F32), vm((GRP, GH, 256), F32), vm((32, 768), F32),
        vm((32, 192), F32),
    ]
    semaphores = [sems(16), sems(6)]
    semaphores += two(7) + two(3) + two(3) + two(7) + two(7) + two(7)
    semaphores += two(5) + two(3) + two(3) + two(2, 7) + two(7) + two(2, 7) + two(2, 7)
    anywhere = pl.BlockSpec(memory_space=pl.ANY)
    outs = pl.pallas_call(
        kernel,
        out_shape=(
            jax.ShapeDtypeStruct((HI, 128), F32),
            jax.ShapeDtypeStruct((32, 8192), F32),
            jax.ShapeDtypeStruct((GRP, GH, 256), F32),
            jax.ShapeDtypeStruct((32, 768), F32),
            jax.ShapeDtypeStruct((32, 192), F32),
        ),
        in_specs=[pl.BlockSpec(memory_space=pltpu.HBM)] * 10,
        out_specs=(anywhere,) * 5,
        scratch_shapes=local + exchanged + results + semaphores,
        compiler_params=pltpu.CompilerParams(
            collective_id=0, has_side_effects=True, vmem_limit_bytes=64 * 2**20
        ),
        name="step",
    )(
        teacher_in, teacher_fc1, teacher_fc2, tok_in.T, enc_proj.T, codes.reshape(1, ROWS),
        ema_count.reshape(HI, 128), ema_sum, dec_in, head,
    )
    outs = pl.pallas_call(
        copy_out,
        out_shape=tuple(jax.ShapeDtypeStruct(o.shape, o.dtype) for o in outs),
        in_specs=[pl.BlockSpec(memory_space=pltpu.HBM)] * 5,
        out_specs=(pl.BlockSpec(memory_space=pltpu.HBM),) * 5,
        scratch_shapes=[vm(o.shape, o.dtype) for o in outs] + two(11),
        compiler_params=pltpu.CompilerParams(vmem_limit_bytes=64 * 2**20),
        name="results",
    )(*outs)
    return (outs[0].reshape(8192), outs[1], outs[2].reshape(768, 256), outs[3], outs[4].T)


def solution(mesh):
    placed = (
        P("dp", None),
        P(None, "mp"),
        P("mp", None),
        P("dp", "mp"),
        P("mp", None),
        P("dp"),
        P(),
        P(),
        P(),
        P(None, "mp"),
    )
    return jax.shard_map(
        on_device,
        mesh=mesh,
        in_specs=placed,
        out_specs=(P(), P(), P(None, "mp"), P(), P("mp", None)),
        check_vma=False,
    )
```

```python
import functools
import math

import jax
import jax.numpy as jnp
from jax import lax
from jax.experimental import pallas as pl
from jax.experimental.pallas import tpu as pltpu
from jax.sharding import PartitionSpec as P

DECAY = 0.5
BETA = 0.25
EPS = 1e-06
MESH = pl.DeviceIdType.MESH
F32 = jnp.float32
BF16 = jnp.bfloat16
GELU_A = math.sqrt(2.0 / math.pi)
GELU_B = 0.044715

NMP = 4
GRP = 8
ZED = 8
ROWS = 256
OWN = 64
HI = 64
QHI = 16
SROW = 64
CROW = 16
GH = 96
GX = 16
GA = 48
SPLIT = 272
FAR = (6, 2, 5, 7, 4, 1, 3)
FAR_Z = (4, 3, 5, 2, 6, 1, 7)


def gelu(x):
    return 0.5 * x * (1.0 + jnp.tanh(GELU_A * (x + GELU_B * (x * x * x))))


def gelu_and_slope(x):
    square = x * x
    t = jnp.tanh(GELU_A * (x + GELU_B * (square * x)))
    value = 0.5 * x * (1.0 + t)
    slope = 0.5 * (1.0 + t) + (0.5 * GELU_A) * x * (1.0 - t * t) * (
        1.0 + (3.0 * GELU_B) * square
    )
    return value, slope


def split_counts(counts):
    upper = counts.astype(BF16)
    return jnp.concatenate([upper, (counts - upper.astype(F32)).astype(BF16)], axis=0)


def join_counts(parts):
    return parts[0:CROW].astype(F32) + parts[CROW:2 * CROW].astype(F32)


def add_sums(parts):
    total = parts[0].astype(F32)
    for part in parts[1:]:
        total = total + part.astype(F32)
    counts = split_counts(total[SROW:SROW + CROW] + total[SROW + CROW:SROW + 2 * CROW])
    return total[0:SROW].astype(BF16), counts


def dot(a, b, ca=1, cb=0):
    return lax.dot_general(a, b, (((ca,), (cb,)), ((), ())), preferred_element_type=F32)


def kernel(
    tin_h, fc1_h, fc2_h, tok_h, enc_h, codes_h, cnt_h, sum_h, dec_h, head_h,
    ncount_h, nsum_h, grads_h,
    tin, fc1, fc2, tok, enc, codes, cnt, esum, dec,
    th, tp, hid_t, q_rows, book, pred,
    hd, tp_r, z_s, z_r, s_s, s_r, s_z, s_all, dp_s, dp_r, dpre, g_s, g_r, g_z, g_all,
    o_count, o_sum,
    ring, load_sem, out_sem,
    hd_ss, hd_rs, tp_ss, tp_rs, z_ss, z_rs, s1_ss, s1_rs, s2_ss, s2_rs, s3_ss, s3_rs,
    s4_ss, s4_rs, dp_ss, dp_rs, dr_ss, dr_rs, g1_ss, g1_rs, x1_ss, x1_rs, g2_ss, g2_rs,
    g3_ss, g3_rs,
):
    dp = lax.axis_index("dp")
    mp = lax.axis_index("mp")
    zed = lax.div(dp, GRP)
    grp = lax.rem(dp, GRP)
    sib = mp + 1 - 2 * lax.rem(mp, 2)
    over = lax.rem(mp + 2, NMP)
    sib_over = lax.rem(sib + 2, NMP)

    def mp_peer(r):
        return (dp, lax.rem(mp + r, NMP))

    def grp_index(k):
        return lax.rem(grp + k, GRP)

    def grp_peer(k):
        return (zed * GRP + grp_index(k), mp)

    def zed_peer(k):
        return (lax.rem(zed + k, ZED) * GRP + grp, mp)

    wrap = (zed * GRP + grp_index(4), over)

    sent = []

    def remote(src, dst, ss, rs, dev):
        c = pltpu.make_async_remote_copy(
            src_ref=src, dst_ref=dst, send_sem=ss, recv_sem=rs,
            device_id=dev, device_id_type=MESH,
        )
        sent.append(c)
        return c

    barrier = pltpu.get_barrier_semaphore()
    yy = lax.rem(grp, 4)
    row = zed * GRP + grp - yy
    near = [mp_peer(r) for r in (1, 2, 3)] + [wrap]
    near += [(row + lax.rem(yy + k, 4), mp) for k in (1, 3)] + [zed_peer(k) for k in (1, ZED - 1)]

    def greet(sem):
        for dev in near:
            pl.semaphore_signal(sem, inc=1, device_id=dev, device_id_type=MESH)

    def hear(sem):
        pl.semaphore_wait(sem, len(near))

    greet(barrier)

    loads = []

    def load(src, dst):
        c = pltpu.make_async_copy(src, dst, load_sem.at[len(loads)])
        c.start()
        loads.append(c)
        return c

    l_tok = load(tok_h, tok)
    l_enc = load(enc_h, enc)
    l_tin = load(tin_h, tin)
    l_fc1 = [load(fc1_h.at[:, pl.ds(n * 256, 256)], fc1.at[n]) for n in range(4)]
    l_head = load(head_h, hd.at[mp])
    l_fc2 = [load(fc2_h.at[:, pl.ds(n * 256, 256)], fc2.at[n]) for n in range(4)]
    l_codes = load(codes_h, codes)
    l_cnt = load(cnt_h, cnt)
    l_sum = load(sum_h, esum)
    l_dec = load(dec_h, dec)

    l_tin.wait()
    for n in range(4):
        l_fc1[n].wait()
        th[:, n * 256:(n + 1) * 256] = gelu(dot(tin[...], fc1[n])).astype(BF16)

    l_tok.wait()
    l_enc.wait()
    z_s[...] = dot(enc[...], tok[...]).astype(BF16)
    l_head.wait()

    hear(barrier)
    greet(ring.at[0])
    c_z = [
        remote(z_s, z_r.at[r - 1], z_ss.at[r - 1], z_rs.at[r - 1], mp_peer(r)) for r in (2, 1, 3)
    ]
    for c in c_z:
        c.start()
    cuts = (pl.ds(0, 320), pl.ds(320, 320), pl.ds(640, 128))
    c_wrap = []
    for i, dev in enumerate((wrap, wrap, (dp, over))):
        c_wrap.append(
            remote(hd.at[mp, cuts[i]], hd.at[mp, cuts[i]], hd_ss.at[i], hd_rs.at[i], dev)
        )
    for c in c_wrap:
        c.start()
    c_sib = remote(hd.at[mp], hd.at[mp], hd_ss.at[3], hd_rs.at[3], (dp, sib))
    c_sib.start()

    for n in range(4):
        l_fc2[n].wait()
        tp[n] = dot(th[...], fc2[n]).astype(BF16)
    c_tp = []
    for r in (2, 1, 3):
        rows = pl.ds(pl.multiple_of(lax.rem(mp + r, NMP) * OWN, OWN), OWN)
        c = remote(
            tp.at[:, rows], tp_r.at[r - 1], tp_ss.at[r - 1], tp_rs.at[r - 1], mp_peer(r)
        )
        c.start()
        c_tp.append(c)

    hear(ring.at[0])
    greet(ring.at[1])

    l_codes.wait()
    code = jnp.broadcast_to(codes[...], (32, ROWS))
    code_hi = jnp.right_shift(code, 7)
    code_lo = jnp.broadcast_to(jnp.bitwise_and(codes[...], 127), (128, ROWS))
    lo_id = lax.broadcasted_iota(jnp.int32, (128, ROWS), 0)
    lo_hot = jnp.where(lo_id == code_lo, 1.0, 0.0).astype(BF16)

    hear(ring.at[1])
    greet(ring.at[2])

    for c in c_z:
        c.wait_recv()
    z_t = z_s[...].astype(F32)
    for r in range(3):
        z_t = z_t + z_r[r].astype(F32)
    for i in range(QHI // 2):
        pair = [jnp.where(code_hi == mp * QHI + i * 2 + j, z_t, 0.0) for j in range(2)]
        pair = jnp.concatenate(pair, axis=0).astype(BF16)
        s_s[i, 0:SROW] = dot(pair, lo_hot, 1, 1).astype(BF16)
    hi_id = lax.broadcasted_iota(jnp.int32, (CROW, ROWS), 0) + mp * QHI
    hi_hot = jnp.where(hi_id == code_hi[0:CROW], 1.0, 0.0).astype(BF16)
    counts = split_counts(dot(hi_hot, lo_hot, 1, 1))
    for i in range(GRP):
        s_s[i, SROW:SROW + 2 * CROW] = counts
    hear(ring.at[2])
    c_s1 = []
    for k in FAR:
        c = remote(
            s_s.at[grp_index(k)], s_r.at[k - 1], s1_ss.at[k - 1], s1_rs.at[k - 1], grp_peer(k)
        )
        c.start()
        c_s1.append(c)

    l_cnt.wait()
    l_sum.wait()
    l_dec.wait()
    lo_twice = jnp.concatenate([lo_hot, lo_hot], axis=0)
    inv = 1.0 / cnt[...]
    for h in range(HI):
        part = esum[:, h * 128:(h + 1) * 128] * inv[h:h + 1, :]
        upper = part.astype(BF16)
        book[h * 32:(h + 1) * 32, 0:128] = upper
        book[h * 32:(h + 1) * 32, 128:256] = (part - upper.astype(F32)).astype(BF16)
    q_t = jnp.zeros((32, ROWS), F32)
    for i in range(HI // 8):
        found = dot(book[i * 256:(i + 1) * 256, :], lo_twice)
        for j in range(8):
            q_t = q_t + jnp.where(code_hi == i * 8 + j, found[j * 32:(j + 1) * 32], 0.0)
    q_rows[...] = q_t.T
    q_round_t = q_t.astype(BF16)
    own_rows = pl.ds(pl.multiple_of(mp * OWN, OWN), OWN)
    hidden, slope = gelu_and_slope(dot(q_rows[own_rows, :].astype(BF16), dec[...]))
    hidden = hidden.astype(BF16)

    c_sib.wait_recv()
    c_fwd = []
    for i in range(3):
        c_wrap[i].wait_recv()
        rows = hd.at[over, cuts[i]]
        c = remote(rows, rows, hd_ss.at[4 + i], hd_rs.at[4 + i], (dp, sib))
        c.start()
        c_fwd.append(c)
    for b in (mp, sib, over):
        pred[b] = dot(hidden, hd[b])
    for c in c_fwd:
        c.wait_recv()
    pred[sib_over] = dot(hidden, hd[sib_over])

    for c in c_tp:
        c.wait_recv()
    target = []
    for n in range(4):
        t = tin[own_rows, n * 256:(n + 1) * 256].astype(F32) + tp[n, own_rows, :].astype(F32)
        for r in range(3):
            t = t + tp_r[r, n].astype(F32)
        target.append(t)
    pp = jnp.zeros((OWN, 256), F32)
    pt = jnp.zeros((OWN, 256), F32)
    tt = jnp.zeros((OWN, 256), F32)
    for n in range(4):
        pp = pp + pred[n] * pred[n]
        pt = pt + pred[n] * target[n]
        tt = tt + target[n] * target[n]
    pp = jnp.sum(pp, axis=1, keepdims=True) + EPS
    pt = jnp.sum(pt, axis=1, keepdims=True)
    tt = jnp.sum(tt, axis=1, keepdims=True) + EPS
    inverse = 1.0 / (jnp.sqrt(pp) * jnp.sqrt(tt))
    scale = pt * inverse / pp
    for n in range(4):
        dp_s[n] = (scale * pred[n] - inverse * target[n]).astype(BF16)
    c_dp = []
    for r in (2, 1, 3):
        c = remote(
            dp_s.at[lax.rem(mp + r, NMP)], dp_r.at[mp], dp_ss.at[r - 1], dp_rs.at[r - 1],
            mp_peer(r),
        )
        c.start()
        c_dp.append(c)
    dp_r[mp] = dp_s[mp]
    dh = dot(dp_s[0], hd[0], 1, 1)
    for n in range(1, 4):
        dh = dh + dot(dp_s[n], hd[n], 1, 1)
    dpre[mp] = (dh * slope).astype(BF16)
    c_dr = []
    for r in (2, 1, 3):
        c = remote(dpre.at[mp], dpre.at[mp], dr_ss.at[r - 1], dr_rs.at[r - 1], mp_peer(r))
        c.start()
        c_dr.append(c)

    for c in c_s1:
        c.wait_recv()
    sums, counts = add_sums([s_s[grp]] + [s_r[k] for k in range(GRP - 1)])
    s_z[zed, 0:SROW] = sums
    s_z[zed, SROW:SROW + 2 * CROW] = counts
    c_s2 = []
    for k in FAR_Z:
        c = remote(s_z.at[zed], s_z.at[zed], s2_ss.at[k - 1], s2_rs.at[k - 1], zed_peer(k))
        c.start()
        c_s2.append(c)

    dec_t = dec[...].astype(F32).T.astype(BF16)
    for n in range(3):
        hid_t[n * 256:(n + 1) * 256, :] = gelu(
            dot(dec_t[n * 256:(n + 1) * 256], q_round_t)
        ).astype(BF16)

    for c in c_dp:
        c.wait_recv()
    grad = dot(hid_t[...], dp_r[...].reshape(ROWS, 256)).astype(BF16)
    for i in range(GRP):
        g_s[i, 0:GH] = grad[i * GH:(i + 1) * GH]
    c_g1 = [[], []]
    for part, rows in enumerate((pl.ds(0, GA), pl.ds(GA, GH - GA))):
        for k in FAR:
            c = remote(
                g_s.at[grp_index(k), rows], g_r.at[k - 1, rows],
                g1_ss.at[part, k - 1], g1_rs.at[part, k - 1], grp_peer(k),
            )
            c.start()
            c_g1[part].append(c)

    for c in c_dr:
        c.wait_recv()
    dpre_all = dpre[...].reshape(ROWS, 768)
    dq_t = dot(dec[...], dpre_all, 1, 1)
    dz_t = (dq_t + 2.0 * BETA * (z_t - q_t)).astype(BF16)
    grad_dec = dot(q_round_t, dpre_all).astype(BF16)
    grad_enc = dot(dz_t, tok[...], 1, 1).astype(BF16)
    for n in range(3):
        for i in range(2):
            g_s[n * 2 + i, GH:GH + GX] = grad_dec[i * 16:(i + 1) * 16, n * 256:(n + 1) * 256]
    for i in range(2):
        g_s[6 + i, GH:GH + GX, 0:192] = grad_enc[i * 16:(i + 1) * 16]
        g_s[6 + i, GH:GH + GX, 192:256] = jnp.zeros((GX, 64), BF16)
    c_x1 = []
    for k in FAR:
        c = remote(
            g_s.at[grp_index(k), pl.ds(GH, GX)], g_r.at[k - 1, pl.ds(GH, GX)],
            x1_ss.at[k - 1], x1_rs.at[k - 1], grp_peer(k),
        )
        c.start()
        c_x1.append(c)

    halves = ((0, GA), (GA, GH + GX - GA))
    c_g2 = [[], []]
    c_g3 = [[], []]

    def along_z(part):
        first, size = halves[part]
        g_part = g_s[grp, first:first + size].astype(F32)
        for k in range(GRP - 1):
            g_part = g_part + g_r[k, first:first + size].astype(F32)
        g_z[zed, first:first + size] = g_part.astype(BF16)
        for k in FAR_Z:
            rows = g_z.at[zed, pl.ds(first, size)]
            c = remote(rows, rows, g2_ss.at[part, k - 1], g2_rs.at[part, k - 1], zed_peer(k))
            c.start()
            c_g2[part].append(c)

    def gather(part):
        first, size = halves[part]
        for c in c_g2[part]:
            c.wait_recv()
        g_part = g_z[0, first:first + size].astype(F32)
        for k in range(1, ZED):
            g_part = g_part + g_z[k, first:first + size].astype(F32)
        g_all[grp, first:first + size] = g_part.astype(BF16)
        for k in FAR:
            rows = g_all.at[grp, pl.ds(first, size)]
            c = remote(rows, rows, g3_ss.at[part, k - 1], g3_rs.at[part, k - 1], grp_peer(k))
            c.start()
            c_g3[part].append(c)

    for c in c_g1[0]:
        c.wait_recv()
    along_z(0)

    for c in c_s2:
        c.wait_recv()
    sums, counts = add_sums([s_z[k] for k in range(ZED)])
    own_part = pl.ds(pl.multiple_of(grp * SROW, SROW), SROW)
    s_all[mp, own_part] = sums
    s_all[mp, pl.ds(GRP * SROW, 2 * CROW)] = counts
    c_s3 = []
    for k in FAR:
        c = remote(
            s_all.at[mp, own_part], s_all.at[mp, own_part], s3_ss.at[k - 1], s3_rs.at[k - 1],
            grp_peer(k),
        )
        c.start()
        c_s3.append(c)

    for c in c_g1[1] + c_x1:
        c.wait_recv()
    along_z(1)
    gather(0)

    for c in c_s3:
        c.wait_recv()
    parts = (pl.ds(0, SPLIT), pl.ds(SPLIT, GRP * SROW + 2 * CROW - SPLIT))
    c_over = []
    for i, dev in enumerate(((dp, over), wrap)):
        rows = s_all.at[mp, parts[i]]
        c = remote(rows, rows, s4_ss.at[i], s4_rs.at[i], dev)
        c.start()
        c_over.append(c)
    c_near = remote(s_all.at[mp], s_all.at[mp], s4_ss.at[2], s4_rs.at[2], (dp, sib))
    c_near.start()

    gather(1)
    c_last = []
    for i in range(2):
        c_over[i].wait_recv()
        rows = s_all.at[over, parts[i]]
        c = remote(rows, rows, s4_ss.at[3 + i], s4_rs.at[3 + i], (dp, sib))
        c.start()
        c_last.append(c)

    for c in c_last + [c_near]:
        c.wait_recv()
    outs = []

    def store(src, dst):
        c = pltpu.make_async_copy(src, dst, out_sem.at[len(outs)])
        c.start()
        outs.append(c)

    for m in range(NMP):
        o_count[m * CROW:(m + 1) * CROW] = (
            DECAY * cnt[m * CROW:(m + 1) * CROW]
            + (1.0 - DECAY) * join_counts(s_all[m, GRP * SROW:GRP * SROW + 2 * CROW])
        )
        for i in range(QHI):
            columns = slice((m * QHI + i) * 128, (m * QHI + i + 1) * 128)
            o_sum[:, columns] = DECAY * esum[:, columns] + (1.0 - DECAY) * s_all[
                m, i * 32:(i + 1) * 32
            ].astype(F32)
    store(o_count, ncount_h)
    store(o_sum, nsum_h)

    for part, (first, size) in enumerate(halves):
        for c in c_g3[part]:
            c.wait_recv()
        rows = pl.ds(first, size)
        store(g_all.at[:, rows], grads_h.at[:, rows])
    for c in sent:
        c.wait_send()
    for c in outs:
        c.wait()


def results(
    count_h, sum_h, grads_h, ncount_h, nsum_h, ghead_h, gdec_h, genc_h,
    count, sums, grads, head, dec, enc, in_sem, out_sem,
):
    groups = [pl.ds(i * 2, 2) for i in range(GRP // 2)]
    columns = [pl.ds(i * 2048, 2048) for i in range(4)]
    ins = [(grads_h.at[g], grads.at[g]) for g in groups]
    ins += [(sum_h.at[:, c], sums.at[:, c]) for c in columns] + [(count_h, count)]
    ins = [pltpu.make_async_copy(*pair, in_sem.at[i]) for i, pair in enumerate(ins)]
    for c in ins:
        c.start()
    outs = []

    def store(src, dst):
        c = pltpu.make_async_copy(src, dst, out_sem.at[len(outs)])
        c.start()
        outs.append(c)

    for i, g in enumerate(groups):
        ins[i].wait()
        for j in (2 * i, 2 * i + 1):
            head[j] = grads[j, 0:GH].astype(F32)
        store(head.at[g], ghead_h.at[g])
    for i, c in enumerate(columns):
        ins[4 + i].wait()
        store(sums.at[:, c], nsum_h.at[:, c])
    ins[8].wait()
    store(count, ncount_h)
    for n in range(3):
        for i in range(2):
            dec[i * 16:(i + 1) * 16, n * 256:(n + 1) * 256] = grads[
                n * 2 + i, GH:GH + GX
            ].astype(F32)
    store(dec, gdec_h)
    for i in range(2):
        enc[i * 16:(i + 1) * 16] = grads[6 + i, GH:GH + GX, 0:192].astype(F32)
    store(enc, genc_h)
    for c in outs:
        c.wait()


def on_device(
    teacher_in, teacher_fc1, teacher_fc2, tok_in, enc_proj, codes, ema_count, ema_sum, dec_in, head
):
    def sems(*shape):
        return pltpu.SemaphoreType.DMA(shape)

    def two(*shape):
        return [sems(*shape), sems(*shape)]

    vm = pltpu.VMEM
    local = [
        vm((ROWS, 1024), BF16), vm((4, 1024, 256), BF16), vm((4, 1024, 256), BF16),
        vm((192, ROWS), BF16), vm((32, 192), BF16), vm((1, ROWS), jnp.int32),
        vm((HI, 128), F32), vm((32, 8192), F32), vm((32, 768), BF16),
        vm((ROWS, 1024), BF16), vm((4, ROWS, 256), BF16), vm((768, ROWS), BF16),
        vm((ROWS, 32), F32), vm((HI * 32, 256), BF16), vm((4, OWN, 256), F32),
    ]
    exchanged = [
        vm((4, 768, 256), BF16), vm((3, 4, OWN, 256), BF16), vm((32, ROWS), BF16),
        vm((3, 32, ROWS), BF16),
        vm((GRP, SROW + 2 * CROW, 128), BF16), vm((GRP - 1, SROW + 2 * CROW, 128), BF16),
        vm((ZED, SROW + 2 * CROW, 128), BF16), vm((NMP, GRP * SROW + 2 * CROW, 128), BF16),
        vm((4, OWN, 256), BF16), vm((4, OWN, 256), BF16), vm((4, OWN, 768), BF16),
        vm((GRP, GH + GX, 256), BF16), vm((GRP - 1, GH + GX, 256), BF16),
        vm((ZED, GH + GX, 256), BF16), vm((GRP, GH + GX, 256), BF16),
    ]
    made = [
        vm((HI, 128), F32), vm((32, 8192), F32),
    ]
    semaphores = [pltpu.SemaphoreType.REGULAR((3,)), sems(16), sems(8)]
    semaphores += two(7) + two(3) + two(3) + two(7) + two(7) + two(7)
    semaphores += two(5) + two(3) + two(3) + two(2, 7) + two(7) + two(2, 7) + two(2, 7)
    anywhere = pl.BlockSpec(memory_space=pl.ANY)
    outs = pl.pallas_call(
        kernel,
        out_shape=(
            jax.ShapeDtypeStruct((HI, 128), F32),
            jax.ShapeDtypeStruct((32, 8192), F32),
            jax.ShapeDtypeStruct((GRP, GH + GX, 256), BF16),
        ),
        in_specs=[pl.BlockSpec(memory_space=pltpu.HBM)] * 10,
        out_specs=(anywhere,) * 3,
        scratch_shapes=local + exchanged + made + semaphores,
        compiler_params=pltpu.CompilerParams(
            collective_id=0, has_side_effects=True, vmem_limit_bytes=64 * 2**20
        ),
        name="step",
    )(
        teacher_in, teacher_fc1, teacher_fc2, tok_in.T, enc_proj.T, codes.reshape(1, ROWS),
        ema_count.reshape(HI, 128), ema_sum, dec_in, head,
    )
    final = [(HI, 128), (32, 8192), (GRP, GH, 256), (32, 768), (32, 192)]
    outs = pl.pallas_call(
        results,
        out_shape=tuple(jax.ShapeDtypeStruct(shape, F32) for shape in final),
        in_specs=[pl.BlockSpec(memory_space=pltpu.HBM)] * 3,
        out_specs=(pl.BlockSpec(memory_space=pltpu.HBM),) * 5,
        scratch_shapes=[vm(final[0], F32), vm(final[1], F32), vm((GRP, GH + GX, 256), BF16)]
        + [vm(shape, F32) for shape in final[2:]]
        + [sems(9), sems(11)],
        compiler_params=pltpu.CompilerParams(vmem_limit_bytes=64 * 2**20),
        name="results",
    )(*outs)
    return (outs[0].reshape(8192), outs[1], outs[2].reshape(768, 256), outs[3], outs[4].T)


def solution(mesh):
    placed = (
        P("dp", None),
        P(None, "mp"),
        P("mp", None),
        P("dp", "mp"),
        P("mp", None),
        P("dp"),
        P(),
        P(),
        P(),
        P(None, "mp"),
    )
    return jax.shard_map(
        on_device,
        mesh=mesh,
        in_specs=placed,
        out_specs=(P(), P(), P(None, "mp"), P(), P("mp", None)),
        check_vma=False,
    )
```

```python
import functools
import math

import jax
import jax.numpy as jnp
from jax import lax
from jax.experimental import pallas as pl
from jax.experimental.pallas import tpu as pltpu
from jax.sharding import PartitionSpec as P

DECAY = 0.5
BETA = 0.25
EPS = 1e-06
MESH = pl.DeviceIdType.MESH
F32 = jnp.float32
BF16 = jnp.bfloat16
GELU_A = math.sqrt(2.0 / math.pi)
GELU_B = 0.044715

NMP = 4
PARTS = 16
QUADS = 4
ROWS = 256
OWN = 64
HI = 64
QHI = 16
CD = 32
SROW = 48
GROW = 48
XROW = 16
OFFSETS = sorted(
    [(z, h, y) for z in range(2) for h in range(2) for y in range(4) if z + h + y > 0],
    key=lambda o: -(o[0] + 2 * o[1] + min(o[2], 4 - o[2])),
)

def gelu(x):
    return 0.5 * x * (1.0 + jnp.tanh(GELU_A * (x + GELU_B * (x * x * x))))


def gelu_and_slope(x):
    square = x * x
    t = jnp.tanh(GELU_A * (x + GELU_B * (square * x)))
    value = 0.5 * x * (1.0 + t)
    slope = 0.5 * (1.0 + t) + (0.5 * GELU_A) * x * (1.0 - t * t) * (
        1.0 + (3.0 * GELU_B) * square
    )
    return value, slope


def count_rows(counts):
    upper = counts.astype(BF16).astype(F32)
    row = lax.broadcasted_iota(jnp.int32, (SROW - CD, 128), 0)
    rest = jnp.where(row == 1, counts - upper, 0.0)
    return jnp.where(row == 0, upper, rest).astype(BF16)


def add_up(parts):
    total = parts[0].astype(F32)
    for part in parts[1:]:
        total = total + part.astype(F32)
    return total


def add_sums(parts):
    total = add_up(parts)
    counts = total[CD:CD + 1] + total[CD + 1:CD + 2]
    return total[0:CD].astype(BF16), count_rows(counts)


def dot(a, b, ca=1, cb=0):
    return lax.dot_general(a, b, (((ca,), (cb,)), ((), ())), preferred_element_type=F32)


def kernel(
    tin_h, fc1_h, fc2_h, tok_h, enc_h, codes_h, cnt_h, sum_h, dec_h, head_h,
    ncount_h, nsum_h, grads_h, small_h,
    tin, fc1, fc2, tok, enc, codes, cnt, esum, dec,
    th, tp, hid_t, q_rows, z_rows, book, pred,
    hd, tp_r, z_s, z_r, s_s, s_r, s_z, s_all, dp_s, dp_r, gd, dz,
    g_s, g_r, g_z, g_all, x_s, x_r, x_z, x_all,
    o_count, o_sum,
    ring, load_sem, out_sem,
    hd_ss, hd_rs, tp_ss, tp_rs, z_ss, z_rs, s1_ss, s1_rs, s2_ss, s2_rs, s3_ss, s3_rs,
    s4_ss, s4_rs, dp_ss, dp_rs, gd_ss, gd_rs, dz_ss, dz_rs, g1_ss, g1_rs, g2_ss, g2_rs,
    g3_ss, g3_rs, x1_ss, x1_rs, x2_ss, x2_rs, x3_ss, x3_rs,
):
    dp = lax.axis_index("dp")
    mp = lax.axis_index("mp")
    zed = lax.div(dp, 8)
    high = lax.rem(lax.div(dp, 4), 2)
    yy = lax.rem(dp, 4)
    odd = lax.rem(zed, 2)
    quad = lax.div(zed, 2)
    part = odd * 8 + high * 4 + yy
    sib = mp + 1 - 2 * lax.rem(mp, 2)
    over = lax.rem(mp + 2, NMP)
    sib_over = lax.rem(sib + 2, NMP)

    def mp_peer(r):
        return (dp, lax.rem(mp + r, NMP))

    def at(z, h, y):
        return z * 8 + h * 4 + y

    part_peers = []
    for dz_, dh_, dy_ in OFFSETS:
        odd_, high_, yy_ = lax.rem(odd + dz_, 2), lax.rem(high + dh_, 2), lax.rem(yy + dy_, 4)
        part_peers.append(((at(quad * 2 + odd_, high_, yy_), mp), at(odd_, high_, yy_)))

    def quad_peer(k):
        return (at(lax.rem(quad + k, QUADS) * 2 + odd, high, yy), mp)

    wrap = (at(zed, 1 - high, yy), over)

    sent = []

    def remote(src, dst, ss, rs, dev):
        c = pltpu.make_async_remote_copy(
            src_ref=src, dst_ref=dst, send_sem=ss, recv_sem=rs,
            device_id=dev, device_id_type=MESH,
        )
        sent.append(c)
        return c

    barrier = pltpu.get_barrier_semaphore()
    near = [mp_peer(r) for r in (1, 2, 3)] + [wrap]
    near += [(at(zed, high, lax.rem(yy + k, 4)), mp) for k in (1, 3)]
    near += [(at(lax.rem(zed + k, 8), high, yy), mp) for k in (1, 7)]

    def greet(sem):
        for dev in near:
            pl.semaphore_signal(sem, inc=1, device_id=dev, device_id_type=MESH)

    def hear(sem):
        pl.semaphore_wait(sem, len(near))

    greet(barrier)

    loads = []

    def load(src, dst):
        c = pltpu.make_async_copy(src, dst, load_sem.at[len(loads)])
        c.start()
        loads.append(c)
        return c

    l_tok = load(tok_h, tok)
    l_enc = load(enc_h, enc)
    l_head = load(head_h, hd.at[mp])
    l_tin = load(tin_h, tin)
    l_fc1 = [load(fc1_h.at[:, pl.ds(n * 256, 256)], fc1.at[n]) for n in range(4)]
    l_fc2 = [load(fc2_h.at[:, pl.ds(n * 256, 256)], fc2.at[n]) for n in range(4)]

    l_tok.wait()
    l_enc.wait()
    z_s[...] = dot(enc[...], tok[...]).astype(BF16)
    l_head.wait()

    hear(barrier)
    greet(ring.at[0])
    c_z = [
        remote(z_s, z_r.at[r - 1], z_ss.at[r - 1], z_rs.at[r - 1], mp_peer(r)) for r in (2, 1, 3)
    ]
    for c in c_z:
        c.start()
    cuts = (pl.ds(0, 256), pl.ds(256, 256), pl.ds(512, 256))
    c_wrap = []
    for i, dev in enumerate((wrap, wrap, (dp, over))):
        c_wrap.append(
            remote(hd.at[mp, cuts[i]], hd.at[mp, cuts[i]], hd_ss.at[i], hd_rs.at[i], dev)
        )
    for c in c_wrap:
        c.start()
    c_sib = remote(hd.at[mp], hd.at[mp], hd_ss.at[3], hd_rs.at[3], (dp, sib))
    c_sib.start()

    l_tin.wait()
    for n in range(4):
        l_fc1[n].wait()
        th[:, n * 256:(n + 1) * 256] = gelu(dot(tin[...], fc1[n])).astype(BF16)
    l_codes = load(codes_h, codes)
    l_cnt = load(cnt_h, cnt)
    l_sum = load(sum_h, esum)
    l_dec = load(dec_h, dec)

    for n in range(4):
        l_fc2[n].wait()
        tp[n] = dot(th[...], fc2[n]).astype(BF16)
    c_tp = []
    for r in (2, 1, 3):
        rows = pl.ds(pl.multiple_of(lax.rem(mp + r, NMP) * OWN, OWN), OWN)
        c = remote(
            tp.at[:, rows], tp_r.at[r - 1], tp_ss.at[r - 1], tp_rs.at[r - 1], mp_peer(r)
        )
        c.start()
        c_tp.append(c)

    hear(ring.at[0])
    greet(ring.at[1])

    l_codes.wait()
    code = jnp.broadcast_to(codes[...], (32, ROWS))
    code_hi = jnp.right_shift(code, 7)
    code_lo = jnp.broadcast_to(jnp.bitwise_and(codes[...], 127), (128, ROWS))
    lo_id = lax.broadcasted_iota(jnp.int32, (128, ROWS), 0)
    lo_hot = jnp.where(lo_id == code_lo, 1.0, 0.0).astype(BF16)

    hear(ring.at[1])
    greet(ring.at[2])

    for c in c_z:
        c.wait_recv()
    z_t = z_s[...].astype(F32)
    for r in range(3):
        z_t = z_t + z_r[r].astype(F32)
    hear(ring.at[2])
    greet(ring.at[3])
    hi_id = lax.broadcasted_iota(jnp.int32, (QHI, ROWS), 0) + mp * QHI
    hi_hot = jnp.where(hi_id == code_hi[0:QHI], 1.0, 0.0).astype(BF16)
    counts = dot(hi_hot, lo_hot, 1, 1)
    for i in range(QHI // 2):
        pair = [jnp.where(code_hi == mp * QHI + i * 2 + j, z_t, 0.0) for j in range(2)]
        pair = dot(jnp.concatenate(pair, axis=0).astype(BF16), lo_hot, 1, 1).astype(BF16)
        for j in range(2):
            s_s[i * 2 + j, 0:CD] = pair[j * CD:(j + 1) * CD]
            s_s[i * 2 + j, CD:SROW] = count_rows(counts[i * 2 + j:i * 2 + j + 1])
    hear(ring.at[3])

    def to_parts(src, dst, ss, rs):
        started = []
        for i, (dev, p) in enumerate(part_peers):
            c = remote(src.at[p], dst.at[i], ss.at[i], rs.at[i], dev)
            c.start()
            started.append(c)
        return started

    def to_quads(buf, ss, rs):
        started = []
        for k in (2, 1, 3):
            c = remote(buf.at[quad], buf.at[quad], ss.at[k - 1], rs.at[k - 1], quad_peer(k))
            c.start()
            started.append(c)
        return started

    def from_part(buf, ss, rs):
        started = []
        for i, (dev, _) in enumerate(part_peers):
            c = remote(buf.at[part], buf.at[part], ss.at[i], rs.at[i], dev)
            c.start()
            started.append(c)
        return started

    def arrive(copies):
        for c in copies:
            c.wait_recv()

    c_s1 = to_parts(s_s, s_r, s1_ss, s1_rs)
    z_rows[...] = z_t.T

    l_cnt.wait()
    l_sum.wait()
    l_dec.wait()
    lo_twice = jnp.concatenate([lo_hot, lo_hot], axis=0)
    inv = 1.0 / cnt[...]
    for h in range(HI):
        vector = esum[:, h * 128:(h + 1) * 128] * inv[h:h + 1, :]
        upper = vector.astype(BF16)
        book[h * 32:(h + 1) * 32, 0:128] = upper
        book[h * 32:(h + 1) * 32, 128:256] = (vector - upper.astype(F32)).astype(BF16)
    q_t = jnp.zeros((32, ROWS), F32)
    for i in range(HI // 8):
        found = dot(book[i * 256:(i + 1) * 256, :], lo_twice)
        for j in range(8):
            q_t = q_t + jnp.where(code_hi == i * 8 + j, found[j * 32:(j + 1) * 32], 0.0)
    q_rows[...] = q_t.T
    q_round_t = q_t.astype(BF16)
    own_rows = pl.ds(pl.multiple_of(mp * OWN, OWN), OWN)
    hidden, slope = gelu_and_slope(dot(q_rows[own_rows, :].astype(BF16), dec[...]))
    hidden = hidden.astype(BF16)

    c_sib.wait_recv()
    c_fwd = []
    for i in range(3):
        c_wrap[i].wait_recv()
        rows = hd.at[over, cuts[i]]
        c = remote(rows, rows, hd_ss.at[4 + i], hd_rs.at[4 + i], (dp, sib))
        c.start()
        c_fwd.append(c)
    for b in (mp, sib, over):
        pred[b] = dot(hidden, hd[b])
    for c in c_fwd:
        c.wait_recv()
    pred[sib_over] = dot(hidden, hd[sib_over])

    for c in c_tp:
        c.wait_recv()
    target = []
    for n in range(4):
        t = tin[own_rows, n * 256:(n + 1) * 256].astype(F32) + tp[n, own_rows, :].astype(F32)
        for r in range(3):
            t = t + tp_r[r, n].astype(F32)
        target.append(t)
    pp = jnp.zeros((OWN, 256), F32)
    pt = jnp.zeros((OWN, 256), F32)
    tt = jnp.zeros((OWN, 256), F32)
    for n in range(4):
        pp = pp + pred[n] * pred[n]
        pt = pt + pred[n] * target[n]
        tt = tt + target[n] * target[n]
    pp = jnp.sum(pp, axis=1, keepdims=True) + EPS
    pt = jnp.sum(pt, axis=1, keepdims=True)
    tt = jnp.sum(tt, axis=1, keepdims=True) + EPS
    inverse = 1.0 / (jnp.sqrt(pp) * jnp.sqrt(tt))
    scale = pt * inverse / pp
    for n in range(4):
        dp_s[n] = (scale * pred[n] - inverse * target[n]).astype(BF16)
    c_dp = []
    for r in (2, 1, 3):
        c = remote(
            dp_s.at[lax.rem(mp + r, NMP)], dp_r.at[mp], dp_ss.at[r - 1], dp_rs.at[r - 1],
            mp_peer(r),
        )
        c.start()
        c_dp.append(c)
    dp_r[mp] = dp_s[mp]
    dh = dot(dp_s[0], hd[0], 1, 1)
    for n in range(1, 4):
        dh = dh + dot(dp_s[n], hd[n], 1, 1)
    dpre = (dh * slope).astype(BF16)

    q_own = q_rows[own_rows, :]
    gd[mp] = dot(q_own.T.astype(BF16), dpre).astype(BF16)
    dq = dot(dpre, dec[...], 1, 1)
    dz[mp] = (dq + 2.0 * BETA * (z_rows[own_rows, :] - q_own)).astype(BF16)
    c_small = []
    for r in (2, 1, 3):
        for buf, ss, rs in ((gd, gd_ss, gd_rs), (dz, dz_ss, dz_rs)):
            c = remote(buf.at[mp], buf.at[mp], ss.at[r - 1], rs.at[r - 1], mp_peer(r))
            c.start()
            c_small.append(c)

    arrive(c_s1)
    sums, counts = add_sums([s_s[part]] + [s_r[i] for i in range(PARTS - 1)])
    s_z[quad, 0:CD] = sums
    s_z[quad, CD:SROW] = counts
    c_s2 = to_quads(s_z, s2_ss, s2_rs)

    dec_t = dec[...].astype(F32).T.astype(BF16)
    for n in range(3):
        hid_t[n * 256:(n + 1) * 256, :] = gelu(
            dot(dec_t[n * 256:(n + 1) * 256], q_round_t)
        ).astype(BF16)

    arrive(c_dp)
    grad = dot(hid_t[...], dp_r[...].reshape(ROWS, 256)).astype(BF16)
    for i in range(PARTS):
        g_s[i] = grad[i * GROW:(i + 1) * GROW]
    c_g1 = to_parts(g_s, g_r, g1_ss, g1_rs)

    arrive(c_small)
    grad_dec = add_up([gd[m] for m in range(NMP)]).astype(BF16)
    dz_t = dz[...].reshape(ROWS, CD).astype(F32).T.astype(BF16)
    grad_enc = dot(dz_t, tok[...], 1, 1).astype(BF16)
    for n in range(6):
        for i in range(2):
            x_s[n * 2 + i] = grad_dec[i * 16:(i + 1) * 16, n * 128:(n + 1) * 128]
    for i in range(2):
        x_s[12 + i] = grad_enc[i * 16:(i + 1) * 16, 0:128]
        x_s[14 + i, :, 0:64] = grad_enc[i * 16:(i + 1) * 16, 128:192]
        x_s[14 + i, :, 64:128] = jnp.zeros((XROW, 64), BF16)
    c_x1 = to_parts(x_s, x_r, x1_ss, x1_rs)

    arrive(c_s2)
    sums, counts = add_sums([s_z[k] for k in range(QUADS)])
    s_all[mp, part, 0:CD] = sums
    s_all[mp, part, CD:SROW] = counts
    c_s3 = from_part(s_all.at[mp], s3_ss, s3_rs)

    arrive(c_g1)
    g_z[quad] = add_up([g_s[part]] + [g_r[i] for i in range(PARTS - 1)]).astype(BF16)
    c_g2 = to_quads(g_z, g2_ss, g2_rs)
    arrive(c_x1)
    x_z[quad] = add_up([x_s[part]] + [x_r[i] for i in range(PARTS - 1)]).astype(BF16)
    c_x2 = to_quads(x_z, x2_ss, x2_rs)

    arrive(c_s3)
    halves = (pl.ds(0, PARTS // 2), pl.ds(PARTS // 2, PARTS // 2))
    c_over = []
    for i, dev in enumerate(((dp, over), wrap)):
        rows = s_all.at[mp, halves[i]]
        c = remote(rows, rows, s4_ss.at[i], s4_rs.at[i], dev)
        c.start()
        c_over.append(c)
    c_near = remote(s_all.at[mp], s_all.at[mp], s4_ss.at[2], s4_rs.at[2], (dp, sib))
    c_near.start()

    arrive(c_g2)
    g_all[part] = add_up([g_z[k] for k in range(QUADS)]).astype(BF16)
    c_g3 = from_part(g_all, g3_ss, g3_rs)
    arrive(c_x2)
    x_all[part] = add_up([x_z[k] for k in range(QUADS)]).astype(BF16)
    c_x3 = from_part(x_all, x3_ss, x3_rs)

    c_last = []
    for i in range(2):
        c_over[i].wait_recv()
        rows = s_all.at[over, halves[i]]
        c = remote(rows, rows, s4_ss.at[3 + i], s4_rs.at[3 + i], (dp, sib))
        c.start()
        c_last.append(c)

    arrive(c_last + [c_near])
    outs = []

    def store(src, dst):
        c = pltpu.make_async_copy(src, dst, out_sem.at[len(outs)])
        c.start()
        outs.append(c)

    for m in range(NMP):
        for i in range(QHI):
            h = m * QHI + i
            columns = slice(h * 128, (h + 1) * 128)
            o_sum[:, columns] = DECAY * esum[:, columns] + (1.0 - DECAY) * s_all[
                m, i, 0:CD
            ].astype(F32)
            rows = s_all[m, i, CD:SROW].astype(F32)
            o_count[h:h + 1] = DECAY * cnt[h:h + 1] + (1.0 - DECAY) * (rows[0:1] + rows[1:2])
    store(o_count, ncount_h)
    store(o_sum, nsum_h)

    arrive(c_g3)
    store(g_all, grads_h)
    arrive(c_x3)
    store(x_all, small_h)
    for c in sent:
        c.wait_send()
    for c in outs:
        c.wait()


def results(
    count_h, sum_h, grads_h, small_h, ncount_h, nsum_h, ghead_h, gdec_h, genc_h,
    count, sums, grads, small, head, dec, enc, in_sem, out_sem,
):
    parts = [pl.ds(i * 4, 4) for i in range(PARTS // 4)]
    columns = [pl.ds(i * 2048, 2048) for i in range(4)]
    ins = [(grads_h.at[p], grads.at[p]) for p in parts] + [(small_h, small)]
    ins += [(sum_h.at[:, c], sums.at[:, c]) for c in columns] + [(count_h, count)]
    ins = [pltpu.make_async_copy(*pair, in_sem.at[i]) for i, pair in enumerate(ins)]
    for c in ins:
        c.start()
    outs = []

    def store(src, dst):
        c = pltpu.make_async_copy(src, dst, out_sem.at[len(outs)])
        c.start()
        outs.append(c)

    for i, p in enumerate(parts):
        ins[i].wait()
        head[p] = grads[p].astype(F32)
        store(head.at[p], ghead_h.at[p])
    ins[4].wait()
    for n in range(6):
        for i in range(2):
            dec[i * 16:(i + 1) * 16, n * 128:(n + 1) * 128] = small[n * 2 + i].astype(F32)
    store(dec, gdec_h)
    for i in range(2):
        enc[i * 16:(i + 1) * 16, 0:128] = small[12 + i].astype(F32)
        enc[i * 16:(i + 1) * 16, 128:192] = small[14 + i, :, 0:64].astype(F32)
    store(enc, genc_h)
    for i, c in enumerate(columns):
        ins[5 + i].wait()
        store(sums.at[:, c], nsum_h.at[:, c])
    ins[9].wait()
    store(count, ncount_h)
    for c in outs:
        c.wait()


def on_device(
    teacher_in, teacher_fc1, teacher_fc2, tok_in, enc_proj, codes, ema_count, ema_sum, dec_in, head
):
    def sems(*shape):
        return pltpu.SemaphoreType.DMA(shape)

    def two(*shape):
        return [sems(*shape), sems(*shape)]

    vm = pltpu.VMEM
    local = [
        vm((ROWS, 1024), BF16), vm((4, 1024, 256), BF16), vm((4, 1024, 256), BF16),
        vm((192, ROWS), BF16), vm((CD, 192), BF16), vm((1, ROWS), jnp.int32),
        vm((HI, 128), F32), vm((CD, 8192), F32), vm((CD, 768), BF16),
        vm((ROWS, 1024), BF16), vm((4, ROWS, 256), BF16), vm((768, ROWS), BF16),
        vm((ROWS, CD), F32), vm((ROWS, CD), F32), vm((HI * CD, 256), BF16),
        vm((4, OWN, 256), F32),
    ]
    exchanged = [
        vm((4, 768, 256), BF16), vm((3, 4, OWN, 256), BF16), vm((CD, ROWS), BF16),
        vm((3, CD, ROWS), BF16),
        vm((PARTS, SROW, 128), BF16), vm((PARTS - 1, SROW, 128), BF16),
        vm((QUADS, SROW, 128), BF16), vm((NMP, PARTS, SROW, 128), BF16),
        vm((4, OWN, 256), BF16), vm((4, OWN, 256), BF16),
        vm((NMP, CD, 768), BF16), vm((NMP, OWN, CD), BF16),
        vm((PARTS, GROW, 256), BF16), vm((PARTS - 1, GROW, 256), BF16),
        vm((QUADS, GROW, 256), BF16), vm((PARTS, GROW, 256), BF16),
        vm((PARTS, XROW, 128), BF16), vm((PARTS - 1, XROW, 128), BF16),
        vm((QUADS, XROW, 128), BF16), vm((PARTS, XROW, 128), BF16),
    ]
    made = [vm((HI, 128), F32), vm((CD, 8192), F32)]
    semaphores = [pltpu.SemaphoreType.REGULAR((4,)), sems(16), sems(4)]
    semaphores += two(7) + two(3) + two(3) + two(15) + two(3) + two(15)
    semaphores += two(5) + two(3) + two(3) + two(3) + two(15) + two(3)
    semaphores += two(15) + two(15) + two(3) + two(15)
    anywhere = pl.BlockSpec(memory_space=pl.ANY)
    outs = pl.pallas_call(
        kernel,
        out_shape=(
            jax.ShapeDtypeStruct((HI, 128), F32),
            jax.ShapeDtypeStruct((32, 8192), F32),
            jax.ShapeDtypeStruct((PARTS, GROW, 256), BF16),
            jax.ShapeDtypeStruct((PARTS, XROW, 128), BF16),
        ),
        in_specs=[pl.BlockSpec(memory_space=pltpu.HBM)] * 10,
        out_specs=(anywhere,) * 4,
        scratch_shapes=local + exchanged + made + semaphores,
        compiler_params=pltpu.CompilerParams(
            collective_id=0, has_side_effects=True, vmem_limit_bytes=64 * 2**20
        ),
        name="step",
    )(
        teacher_in, teacher_fc1, teacher_fc2, tok_in.T, enc_proj.T, codes.reshape(1, ROWS),
        ema_count.reshape(HI, 128), ema_sum, dec_in, head,
    )
    final = [(HI, 128), (CD, 8192), (PARTS, GROW, 256), (CD, 768), (CD, 192)]
    outs = pl.pallas_call(
        results,
        out_shape=tuple(jax.ShapeDtypeStruct(shape, F32) for shape in final),
        in_specs=[pl.BlockSpec(memory_space=pltpu.HBM)] * 4,
        out_specs=(pl.BlockSpec(memory_space=pltpu.HBM),) * 5,
        scratch_shapes=[vm(final[0], F32), vm(final[1], F32)]
        + [vm((PARTS, GROW, 256), BF16), vm((PARTS, XROW, 128), BF16)]
        + [vm(shape, F32) for shape in final[2:]]
        + [sems(10), sems(11)],
        compiler_params=pltpu.CompilerParams(vmem_limit_bytes=64 * 2**20),
        name="results",
    )(*outs)
    return (outs[0].reshape(8192), outs[1], outs[2].reshape(768, 256), outs[3], outs[4].T)


def solution(mesh):
    placed = (
        P("dp", None),
        P(None, "mp"),
        P("mp", None),
        P("dp", "mp"),
        P("mp", None),
        P("dp"),
        P(),
        P(),
        P(),
        P(None, "mp"),
    )
    return jax.shard_map(
        on_device,
        mesh=mesh,
        in_specs=placed,
        out_specs=(P(), P(), P(None, "mp"), P(), P("mp", None)),
        check_vma=False,
    )
```

```python
import functools
import math

import jax
import jax.numpy as jnp
from jax import lax
from jax.experimental import pallas as pl
from jax.experimental.pallas import tpu as pltpu
from jax.sharding import PartitionSpec as P

DECAY = 0.5
BETA = 0.25
EPS = 1e-06
MESH = pl.DeviceIdType.MESH
F32 = jnp.float32
BF16 = jnp.bfloat16
GELU_A = math.sqrt(2.0 / math.pi)
GELU_B = 0.044715

NMP = 4
PARTS = 16
QUADS = 4
ROWS = 256
OWN = 64
HI = 64
QHI = 16
CD = 32
SROW = 48
GROW = 48
XROW = 16
OFFSETS = sorted(
    [(z, h, y) for z in range(2) for h in range(2) for y in range(4) if z + h + y > 0],
    key=lambda o: -(o[0] + 2 * o[1] + min(o[2], 4 - o[2])),
)

def gelu(x):
    return 0.5 * x * (1.0 + jnp.tanh(GELU_A * (x + GELU_B * (x * x * x))))


def gelu_and_slope(x):
    square = x * x
    t = jnp.tanh(GELU_A * (x + GELU_B * (square * x)))
    value = 0.5 * x * (1.0 + t)
    slope = 0.5 * (1.0 + t) + (0.5 * GELU_A) * x * (1.0 - t * t) * (
        1.0 + (3.0 * GELU_B) * square
    )
    return value, slope


def count_rows(counts):
    upper = counts.astype(BF16).astype(F32)
    row = lax.broadcasted_iota(jnp.int32, (SROW - CD, 128), 0)
    rest = jnp.where(row == 1, counts - upper, 0.0)
    return jnp.where(row == 0, upper, rest).astype(BF16)


def add_up(parts):
    total = parts[0].astype(F32)
    for part in parts[1:]:
        total = total + part.astype(F32)
    return total


def add_sums(parts):
    total = add_up(parts)
    counts = total[CD:CD + 1] + total[CD + 1:CD + 2]
    return total[0:CD].astype(BF16), count_rows(counts)


def dot(a, b, ca=1, cb=0):
    return lax.dot_general(a, b, (((ca,), (cb,)), ((), ())), preferred_element_type=F32)


def kernel(
    tin_h, fc1_h, fc2_h, tok_h, enc_h, codes_h, cnt_h, sum_h, dec_h, head_h,
    ncount_h, nsum_h, grads_h, small_h,
    tin, fc1, fc2, tok, enc, codes, cnt, esum, dec,
    th, tp, hid_t, q_rows, z_rows, book, pred,
    hd, tp_s, tp_r, z_s, z_r, s_s, s_r, s_z, s_all, dp_s, dp_r, gd, dz,
    g_s, g_r, g_z, g_all, x_s, x_r, x_z, x_all,
    o_count, o_sum,
    ring, load_sem, out_sem,
    hd_ss, hd_rs, tp_ss, tp_rs, z_ss, z_rs, s1_ss, s1_rs, s2_ss, s2_rs, s3_ss, s3_rs,
    s4_ss, s4_rs, dp_ss, dp_rs, gd_ss, gd_rs, dz_ss, dz_rs, g1_ss, g1_rs, g2_ss, g2_rs,
    g3_ss, g3_rs, x1_ss, x1_rs, x2_ss, x2_rs, x3_ss, x3_rs,
):
    dp = lax.axis_index("dp")
    mp = lax.axis_index("mp")
    zed = lax.div(dp, 8)
    high = lax.rem(lax.div(dp, 4), 2)
    yy = lax.rem(dp, 4)
    odd = lax.rem(zed, 2)
    quad = lax.div(zed, 2)
    part = odd * 8 + high * 4 + yy
    sib = mp + 1 - 2 * lax.rem(mp, 2)
    over = lax.rem(mp + 2, NMP)
    sib_over = lax.rem(sib + 2, NMP)

    def mp_peer(r):
        return (dp, lax.rem(mp + r, NMP))

    def at(z, h, y):
        return z * 8 + h * 4 + y

    part_peers = []
    for dz_, dh_, dy_ in OFFSETS:
        odd_, high_, yy_ = lax.rem(odd + dz_, 2), lax.rem(high + dh_, 2), lax.rem(yy + dy_, 4)
        part_peers.append(((at(quad * 2 + odd_, high_, yy_), mp), at(odd_, high_, yy_)))

    def quad_peer(k):
        return (at(lax.rem(quad + k, QUADS) * 2 + odd, high, yy), mp)

    wrap = (at(zed, 1 - high, yy), over)

    sent = []

    def remote(src, dst, ss, rs, dev):
        c = pltpu.make_async_remote_copy(
            src_ref=src, dst_ref=dst, send_sem=ss, recv_sem=rs,
            device_id=dev, device_id_type=MESH,
        )
        sent.append(c)
        return c

    barrier = pltpu.get_barrier_semaphore()
    near = [mp_peer(r) for r in (1, 2, 3)] + [wrap]
    near += [(at(zed, high, lax.rem(yy + k, 4)), mp) for k in (1, 3)]
    near += [(at(lax.rem(zed + k, 8), high, yy), mp) for k in (1, 7)]

    def greet(sem):
        for dev in near:
            pl.semaphore_signal(sem, inc=1, device_id=dev, device_id_type=MESH)

    def hear(sem):
        pl.semaphore_wait(sem, len(near))

    greet(barrier)

    loads = []

    def load(src, dst):
        c = pltpu.make_async_copy(src, dst, load_sem.at[len(loads)])
        c.start()
        loads.append(c)
        return c

    l_tok = load(tok_h, tok)
    l_enc = load(enc_h, enc)
    l_head = load(head_h, hd.at[mp])
    l_tin = load(tin_h, tin)
    l_fc1 = [load(fc1_h.at[:, pl.ds(n * 256, 256)], fc1.at[n]) for n in range(4)]
    l_fc2 = [load(fc2_h.at[:, pl.ds(n * 256, 256)], fc2.at[n]) for n in range(4)]

    l_tok.wait()
    l_enc.wait()
    z_s[...] = dot(enc[...], tok[...]).astype(BF16)
    l_head.wait()

    hear(barrier)
    greet(ring.at[0])
    c_z = [
        remote(z_s, z_r.at[r - 1], z_ss.at[r - 1], z_rs.at[r - 1], mp_peer(r)) for r in (2, 1, 3)
    ]
    for c in c_z:
        c.start()
    cuts = (pl.ds(0, 224), pl.ds(224, 224), pl.ds(448, 320))
    c_wrap = []
    for i, dev in enumerate((wrap, wrap, (dp, over))):
        c_wrap.append(
            remote(hd.at[mp, cuts[i]], hd.at[mp, cuts[i]], hd_ss.at[i], hd_rs.at[i], dev)
        )
    for c in c_wrap:
        c.start()
    c_sib = remote(hd.at[mp], hd.at[mp], hd_ss.at[3], hd_rs.at[3], (dp, sib))
    c_sib.start()

    l_tin.wait()
    for n in range(4):
        l_fc1[n].wait()
        th[:, n * 256:(n + 1) * 256] = gelu(dot(tin[...], fc1[n])).astype(BF16)
    l_codes = load(codes_h, codes)
    l_cnt = load(cnt_h, cnt)
    l_sum = load(sum_h, esum)
    l_dec = load(dec_h, dec)

    def rows_of(m):
        return pl.ds(pl.multiple_of(m * OWN, OWN), OWN)

    c_tp = []

    def to_core(cols, m, slot, i):
        c = remote(
            tp.at[cols, rows_of(m)], tp_r.at[slot, cols], tp_ss.at[i], tp_rs.at[i], (dp, sib)
        )
        c.start()
        c_tp.append(c)

    pairs = (pl.ds(0, 2), pl.ds(2, 2))
    for i in range(2):
        for n in (2 * i, 2 * i + 1):
            l_fc2[n].wait()
            tp[n] = dot(th[...], fc2[n]).astype(BF16)
        to_core(pairs[i], sib_over, 0, i)
    to_core(pl.ds(0, 4), sib, 1, 2)

    hear(ring.at[0])
    greet(ring.at[1])

    l_codes.wait()
    code = jnp.broadcast_to(codes[...], (32, ROWS))
    code_hi = jnp.right_shift(code, 7)
    code_lo = jnp.broadcast_to(jnp.bitwise_and(codes[...], 127), (128, ROWS))
    lo_id = lax.broadcasted_iota(jnp.int32, (128, ROWS), 0)
    lo_hot = jnp.where(lo_id == code_lo, 1.0, 0.0).astype(BF16)

    c_chip = []
    for i in range(2):
        c_tp[i].wait_recv()
        for n in (2 * i, 2 * i + 1):
            tp_s[n] = (tp[n, rows_of(over), :].astype(F32) + tp_r[0, n].astype(F32)).astype(BF16)
        c = remote(
            tp_s.at[pairs[i]], tp_r.at[2, pairs[i]], tp_ss.at[3 + i], tp_rs.at[3 + i], (dp, over)
        )
        c.start()
        c_chip.append(c)

    hear(ring.at[1])
    greet(ring.at[2])

    for c in c_z:
        c.wait_recv()
    z_t = z_s[...].astype(F32)
    for r in range(3):
        z_t = z_t + z_r[r].astype(F32)
    hi_id = lax.broadcasted_iota(jnp.int32, (QHI, ROWS), 0) + mp * QHI
    hi_hot = jnp.where(hi_id == code_hi[0:QHI], 1.0, 0.0).astype(BF16)
    counts = dot(hi_hot, lo_hot, 1, 1)
    for i in range(QHI // 2):
        pair = [jnp.where(code_hi == mp * QHI + i * 2 + j, z_t, 0.0) for j in range(2)]
        pair = dot(jnp.concatenate(pair, axis=0).astype(BF16), lo_hot, 1, 1).astype(BF16)
        for j in range(2):
            s_s[i * 2 + j, 0:CD] = pair[j * CD:(j + 1) * CD]
            s_s[i * 2 + j, CD:SROW] = count_rows(counts[i * 2 + j:i * 2 + j + 1])
    hear(ring.at[2])
    greet(ring.at[3])

    def to_parts(src, dst, ss, rs):
        started = []
        for i, (dev, p) in enumerate(part_peers):
            c = remote(src.at[p], dst.at[i], ss.at[i], rs.at[i], dev)
            c.start()
            started.append(c)
        return started

    def to_quads(buf, ss, rs):
        started = []
        for k in (2, 1, 3):
            c = remote(buf.at[quad], buf.at[quad], ss.at[k - 1], rs.at[k - 1], quad_peer(k))
            c.start()
            started.append(c)
        return started

    def from_part(buf, ss, rs):
        started = []
        for i, (dev, _) in enumerate(part_peers):
            c = remote(buf.at[part], buf.at[part], ss.at[i], rs.at[i], dev)
            c.start()
            started.append(c)
        return started

    def arrive(copies):
        for c in copies:
            c.wait_recv()

    z_rows[...] = z_t.T

    l_cnt.wait()
    l_sum.wait()
    l_dec.wait()
    lo_twice = jnp.concatenate([lo_hot, lo_hot], axis=0)
    inv = 1.0 / cnt[...]
    for h in range(HI):
        vector = esum[:, h * 128:(h + 1) * 128] * inv[h:h + 1, :]
        upper = vector.astype(BF16)
        book[h * 32:(h + 1) * 32, 0:128] = upper
        book[h * 32:(h + 1) * 32, 128:256] = (vector - upper.astype(F32)).astype(BF16)
    q_t = jnp.zeros((32, ROWS), F32)
    for i in range(HI // 8):
        found = dot(book[i * 256:(i + 1) * 256, :], lo_twice)
        for j in range(8):
            q_t = q_t + jnp.where(code_hi == i * 8 + j, found[j * 32:(j + 1) * 32], 0.0)
    q_rows[...] = q_t.T
    q_round_t = q_t.astype(BF16)
    own_rows = pl.ds(pl.multiple_of(mp * OWN, OWN), OWN)
    hidden, slope = gelu_and_slope(dot(q_rows[own_rows, :].astype(BF16), dec[...]))
    hidden = hidden.astype(BF16)

    hear(ring.at[3])
    c_s1 = to_parts(s_s, s_r, s1_ss, s1_rs)

    c_sib.wait_recv()
    c_fwd = []
    for i in range(3):
        c_wrap[i].wait_recv()
        rows = hd.at[over, cuts[i]]
        c = remote(rows, rows, hd_ss.at[4 + i], hd_rs.at[4 + i], (dp, sib))
        c.start()
        c_fwd.append(c)
    for b in (mp, sib, over):
        pred[b] = dot(hidden, hd[b])
    for c in c_fwd:
        c.wait_recv()
    pred[sib_over] = dot(hidden, hd[sib_over])

    arrive([c_tp[2]] + c_chip)
    target = []
    for n in range(4):
        t = tin[own_rows, n * 256:(n + 1) * 256].astype(F32) + tp[n, own_rows, :].astype(F32)
        t = t + tp_r[1, n].astype(F32) + tp_r[2, n].astype(F32)
        target.append(t)
    pp = jnp.zeros((OWN, 256), F32)
    pt = jnp.zeros((OWN, 256), F32)
    tt = jnp.zeros((OWN, 256), F32)
    for n in range(4):
        pp = pp + pred[n] * pred[n]
        pt = pt + pred[n] * target[n]
        tt = tt + target[n] * target[n]
    pp = jnp.sum(pp, axis=1, keepdims=True) + EPS
    pt = jnp.sum(pt, axis=1, keepdims=True)
    tt = jnp.sum(tt, axis=1, keepdims=True) + EPS
    inverse = 1.0 / (jnp.sqrt(pp) * jnp.sqrt(tt))
    scale = pt * inverse / pp
    for n in range(4):
        dp_s[n] = (scale * pred[n] - inverse * target[n]).astype(BF16)
    c_dp = []
    for r in (2, 1, 3):
        c = remote(
            dp_s.at[lax.rem(mp + r, NMP)], dp_r.at[mp], dp_ss.at[r - 1], dp_rs.at[r - 1],
            mp_peer(r),
        )
        c.start()
        c_dp.append(c)
    dp_r[mp] = dp_s[mp]
    dh = dot(dp_s[0], hd[0], 1, 1)
    for n in range(1, 4):
        dh = dh + dot(dp_s[n], hd[n], 1, 1)
    dpre = (dh * slope).astype(BF16)

    q_own = q_rows[own_rows, :]
    gd[mp] = dot(q_own.T.astype(BF16), dpre).astype(BF16)
    dq = dot(dpre, dec[...], 1, 1)
    dz[mp] = (dq + 2.0 * BETA * (z_rows[own_rows, :] - q_own)).astype(BF16)
    c_small = []
    for r in (2, 1, 3):
        for buf, ss, rs in ((gd, gd_ss, gd_rs), (dz, dz_ss, dz_rs)):
            c = remote(buf.at[mp], buf.at[mp], ss.at[r - 1], rs.at[r - 1], mp_peer(r))
            c.start()
            c_small.append(c)

    arrive(c_s1)
    sums, counts = add_sums([s_s[part]] + [s_r[i] for i in range(PARTS - 1)])
    s_z[quad, 0:CD] = sums
    s_z[quad, CD:SROW] = counts
    c_s2 = to_quads(s_z, s2_ss, s2_rs)

    dec_t = dec[...].astype(F32).T.astype(BF16)
    for n in range(3):
        hid_t[n * 256:(n + 1) * 256, :] = gelu(
            dot(dec_t[n * 256:(n + 1) * 256], q_round_t)
        ).astype(BF16)

    arrive(c_small)
    grad_dec = add_up([gd[m] for m in range(NMP)]).astype(BF16)
    dz_t = dz[...].reshape(ROWS, CD).astype(F32).T.astype(BF16)
    grad_enc = dot(dz_t, tok[...], 1, 1).astype(BF16)
    for n in range(6):
        for i in range(2):
            x_s[n * 2 + i] = grad_dec[i * 16:(i + 1) * 16, n * 128:(n + 1) * 128]
    for i in range(2):
        x_s[12 + i] = grad_enc[i * 16:(i + 1) * 16, 0:128]
        x_s[14 + i, :, 0:64] = grad_enc[i * 16:(i + 1) * 16, 128:192]
        x_s[14 + i, :, 64:128] = jnp.zeros((XROW, 64), BF16)
    c_x1 = to_parts(x_s, x_r, x1_ss, x1_rs)

    arrive(c_dp)
    grad = dot(hid_t[...], dp_r[...].reshape(ROWS, 256)).astype(BF16)
    for i in range(PARTS):
        g_s[i] = grad[i * GROW:(i + 1) * GROW]
    c_g1 = to_parts(g_s, g_r, g1_ss, g1_rs)

    arrive(c_s2)
    sums, counts = add_sums([s_z[k] for k in range(QUADS)])
    s_all[mp, part, 0:CD] = sums
    s_all[mp, part, CD:SROW] = counts
    c_s3 = from_part(s_all.at[mp], s3_ss, s3_rs)

    arrive(c_g1)
    g_z[quad] = add_up([g_s[part]] + [g_r[i] for i in range(PARTS - 1)]).astype(BF16)
    c_g2 = to_quads(g_z, g2_ss, g2_rs)
    arrive(c_x1)
    x_z[quad] = add_up([x_s[part]] + [x_r[i] for i in range(PARTS - 1)]).astype(BF16)
    c_x2 = to_quads(x_z, x2_ss, x2_rs)

    arrive(c_s3)
    halves = (pl.ds(0, PARTS // 2), pl.ds(PARTS // 2, PARTS // 2))
    c_over = []
    for i, dev in enumerate(((dp, over), wrap)):
        rows = s_all.at[mp, halves[i]]
        c = remote(rows, rows, s4_ss.at[i], s4_rs.at[i], dev)
        c.start()
        c_over.append(c)
    c_near = remote(s_all.at[mp], s_all.at[mp], s4_ss.at[2], s4_rs.at[2], (dp, sib))
    c_near.start()

    arrive(c_g2)
    g_all[part] = add_up([g_z[k] for k in range(QUADS)]).astype(BF16)
    c_g3 = from_part(g_all, g3_ss, g3_rs)
    arrive(c_x2)
    x_all[part] = add_up([x_z[k] for k in range(QUADS)]).astype(BF16)
    c_x3 = from_part(x_all, x3_ss, x3_rs)

    c_last = []
    for i in range(2):
        c_over[i].wait_recv()
        rows = s_all.at[over, halves[i]]
        c = remote(rows, rows, s4_ss.at[3 + i], s4_rs.at[3 + i], (dp, sib))
        c.start()
        c_last.append(c)

    arrive(c_last + [c_near])
    outs = []

    def store(src, dst):
        c = pltpu.make_async_copy(src, dst, out_sem.at[len(outs)])
        c.start()
        outs.append(c)

    for m in range(NMP):
        for i in range(QHI):
            h = m * QHI + i
            columns = slice(h * 128, (h + 1) * 128)
            o_sum[:, columns] = DECAY * esum[:, columns] + (1.0 - DECAY) * s_all[
                m, i, 0:CD
            ].astype(F32)
            rows = s_all[m, i, CD:SROW].astype(F32)
            o_count[h:h + 1] = DECAY * cnt[h:h + 1] + (1.0 - DECAY) * (rows[0:1] + rows[1:2])
    store(o_count, ncount_h)
    store(o_sum, nsum_h)

    arrive(c_g3)
    store(g_all, grads_h)
    arrive(c_x3)
    store(x_all, small_h)
    for c in sent:
        c.wait_send()
    for c in outs:
        c.wait()


def results(
    count_h, sum_h, grads_h, small_h, ncount_h, nsum_h, ghead_h, gdec_h, genc_h,
    count, sums, grads, small, head, dec, enc, in_sem, out_sem,
):
    parts = [pl.ds(i * 4, 4) for i in range(PARTS // 4)]
    columns = [pl.ds(i * 2048, 2048) for i in range(4)]
    ins = [(grads_h.at[p], grads.at[p]) for p in parts] + [(small_h, small)]
    ins += [(sum_h.at[:, c], sums.at[:, c]) for c in columns] + [(count_h, count)]
    ins = [pltpu.make_async_copy(*pair, in_sem.at[i]) for i, pair in enumerate(ins)]
    for c in ins:
        c.start()
    outs = []

    def store(src, dst):
        c = pltpu.make_async_copy(src, dst, out_sem.at[len(outs)])
        c.start()
        outs.append(c)

    for i, p in enumerate(parts):
        ins[i].wait()
        head[p] = grads[p].astype(F32)
        store(head.at[p], ghead_h.at[p])
    ins[4].wait()
    for n in range(6):
        for i in range(2):
            dec[i * 16:(i + 1) * 16, n * 128:(n + 1) * 128] = small[n * 2 + i].astype(F32)
    store(dec, gdec_h)
    for i in range(2):
        enc[i * 16:(i + 1) * 16, 0:128] = small[12 + i].astype(F32)
        enc[i * 16:(i + 1) * 16, 128:192] = small[14 + i, :, 0:64].astype(F32)
    store(enc, genc_h)
    for i, c in enumerate(columns):
        ins[5 + i].wait()
        store(sums.at[:, c], nsum_h.at[:, c])
    ins[9].wait()
    store(count, ncount_h)
    for c in outs:
        c.wait()


def on_device(
    teacher_in, teacher_fc1, teacher_fc2, tok_in, enc_proj, codes, ema_count, ema_sum, dec_in, head
):
    def sems(*shape):
        return pltpu.SemaphoreType.DMA(shape)

    def two(*shape):
        return [sems(*shape), sems(*shape)]

    vm = pltpu.VMEM
    local = [
        vm((ROWS, 1024), BF16), vm((4, 1024, 256), BF16), vm((4, 1024, 256), BF16),
        vm((192, ROWS), BF16), vm((CD, 192), BF16), vm((1, ROWS), jnp.int32),
        vm((HI, 128), F32), vm((CD, 8192), F32), vm((CD, 768), BF16),
        vm((ROWS, 1024), BF16), vm((4, ROWS, 256), BF16), vm((768, ROWS), BF16),
        vm((ROWS, CD), F32), vm((ROWS, CD), F32), vm((HI * CD, 256), BF16),
        vm((4, OWN, 256), F32),
    ]
    exchanged = [
        vm((4, 768, 256), BF16), vm((4, OWN, 256), BF16), vm((3, 4, OWN, 256), BF16),
        vm((CD, ROWS), BF16),
        vm((3, CD, ROWS), BF16),
        vm((PARTS, SROW, 128), BF16), vm((PARTS - 1, SROW, 128), BF16),
        vm((QUADS, SROW, 128), BF16), vm((NMP, PARTS, SROW, 128), BF16),
        vm((4, OWN, 256), BF16), vm((4, OWN, 256), BF16),
        vm((NMP, CD, 768), BF16), vm((NMP, OWN, CD), BF16),
        vm((PARTS, GROW, 256), BF16), vm((PARTS - 1, GROW, 256), BF16),
        vm((QUADS, GROW, 256), BF16), vm((PARTS, GROW, 256), BF16),
        vm((PARTS, XROW, 128), BF16), vm((PARTS - 1, XROW, 128), BF16),
        vm((QUADS, XROW, 128), BF16), vm((PARTS, XROW, 128), BF16),
    ]
    made = [vm((HI, 128), F32), vm((CD, 8192), F32)]
    semaphores = [pltpu.SemaphoreType.REGULAR((4,)), sems(16), sems(4)]
    semaphores += two(7) + two(5) + two(3) + two(15) + two(3) + two(15)
    semaphores += two(5) + two(3) + two(3) + two(3) + two(15) + two(3)
    semaphores += two(15) + two(15) + two(3) + two(15)
    anywhere = pl.BlockSpec(memory_space=pl.ANY)
    outs = pl.pallas_call(
        kernel,
        out_shape=(
            jax.ShapeDtypeStruct((HI, 128), F32),
            jax.ShapeDtypeStruct((32, 8192), F32),
            jax.ShapeDtypeStruct((PARTS, GROW, 256), BF16),
            jax.ShapeDtypeStruct((PARTS, XROW, 128), BF16),
        ),
        in_specs=[pl.BlockSpec(memory_space=pltpu.HBM)] * 10,
        out_specs=(anywhere,) * 4,
        scratch_shapes=local + exchanged + made + semaphores,
        compiler_params=pltpu.CompilerParams(
            collective_id=0, has_side_effects=True, vmem_limit_bytes=64 * 2**20
        ),
        name="step",
    )(
        teacher_in, teacher_fc1, teacher_fc2, tok_in.T, enc_proj.T, codes.reshape(1, ROWS),
        ema_count.reshape(HI, 128), ema_sum, dec_in, head,
    )
    final = [(HI, 128), (CD, 8192), (PARTS, GROW, 256), (CD, 768), (CD, 192)]
    outs = pl.pallas_call(
        results,
        out_shape=tuple(jax.ShapeDtypeStruct(shape, F32) for shape in final),
        in_specs=[pl.BlockSpec(memory_space=pltpu.HBM)] * 4,
        out_specs=(pl.BlockSpec(memory_space=pltpu.HBM),) * 5,
        scratch_shapes=[vm(final[0], F32), vm(final[1], F32)]
        + [vm((PARTS, GROW, 256), BF16), vm((PARTS, XROW, 128), BF16)]
        + [vm(shape, F32) for shape in final[2:]]
        + [sems(10), sems(11)],
        compiler_params=pltpu.CompilerParams(vmem_limit_bytes=64 * 2**20),
        name="results",
    )(*outs)
    return (outs[0].reshape(8192), outs[1], outs[2].reshape(768, 256), outs[3], outs[4].T)


def solution(mesh):
    placed = (
        P("dp", None),
        P(None, "mp"),
        P("mp", None),
        P("dp", "mp"),
        P("mp", None),
        P("dp"),
        P(),
        P(),
        P(),
        P(None, "mp"),
    )
    return jax.shard_map(
        on_device,
        mesh=mesh,
        in_specs=placed,
        out_specs=(P(), P(), P(None, "mp"), P(), P("mp", None)),
        check_vma=False,
    )
```

```python
import functools
import math

import jax
import jax.numpy as jnp
from jax import lax
from jax.experimental import pallas as pl
from jax.experimental.pallas import tpu as pltpu
from jax.sharding import PartitionSpec as P

DECAY = 0.5
BETA = 0.25
EPS = 1e-06
MESH = pl.DeviceIdType.MESH
F32 = jnp.float32
BF16 = jnp.bfloat16
GELU_A = math.sqrt(2.0 / math.pi)
GELU_B = 0.044715

NMP = 4
PARTS = 16
QUADS = 4
ROWS = 256
OWN = 64
HI = 64
QHI = 16
CD = 32
SROW = 48
GROW = 48
XROW = 16
OFFSETS = sorted(
    [(z, h, y) for z in range(2) for h in range(2) for y in range(4) if z + h + y > 0],
    key=lambda o: -(o[0] + 2 * o[1] + min(o[2], 4 - o[2])),
)

def gelu(x):
    return 0.5 * x * (1.0 + jnp.tanh(GELU_A * (x + GELU_B * (x * x * x))))


def gelu_and_slope(x):
    square = x * x
    t = jnp.tanh(GELU_A * (x + GELU_B * (square * x)))
    value = 0.5 * x * (1.0 + t)
    slope = 0.5 * (1.0 + t) + (0.5 * GELU_A) * x * (1.0 - t * t) * (
        1.0 + (3.0 * GELU_B) * square
    )
    return value, slope


def count_rows(counts):
    upper = counts.astype(BF16).astype(F32)
    row = lax.broadcasted_iota(jnp.int32, (SROW - CD, 128), 0)
    rest = jnp.where(row == 1, counts - upper, 0.0)
    return jnp.where(row == 0, upper, rest).astype(BF16)


def add_up(parts):
    total = parts[0].astype(F32)
    for part in parts[1:]:
        total = total + part.astype(F32)
    return total


def add_sums(parts):
    total = add_up(parts)
    counts = total[CD:CD + 1] + total[CD + 1:CD + 2]
    return total[0:CD].astype(BF16), count_rows(counts)


def dot(a, b, ca=1, cb=0):
    return lax.dot_general(a, b, (((ca,), (cb,)), ((), ())), preferred_element_type=F32)


def kernel(
    tin_h, fc1_h, fc2_h, tok_h, enc_h, codes_h, cnt_h, sum_h, dec_h, head_h,
    ncount_h, nsum_h, grads_h, small_h,
    tin, fc1, fc2, tok, enc, codes, cnt, esum, dec,
    th, tp, hid_t, q_rows, z_rows, book, pred,
    hd, tp_s, tp_r, z_s, z_r, s_s, s_r, s_z, s_all, dp_s, dp_r, gd, dz,
    g_s, g_r, g_z, g_sum, x_s, x_r, x_z, x_sum,
    o_count, o_sum,
    ring, load_sem, out_sem,
    hd_ss, hd_rs, tp_ss, tp_rs, z_ss, z_rs, s1_ss, s1_rs, s2_ss, s2_rs, s3_ss, s3_rs,
    s4_ss, s4_rs, dp_ss, dp_rs, gd_ss, gd_rs, dz_ss, dz_rs, g1_ss, g1_rs, g2_ss, g2_rs,
    g3_ss, g3_rs, x1_ss, x1_rs, x2_ss, x2_rs, x3_ss, x3_rs,
):
    dp = lax.axis_index("dp")
    mp = lax.axis_index("mp")
    zed = lax.div(dp, 8)
    high = lax.rem(lax.div(dp, 4), 2)
    yy = lax.rem(dp, 4)
    odd = lax.rem(zed, 2)
    quad = lax.div(zed, 2)
    part = odd * 8 + high * 4 + yy
    sib = mp + 1 - 2 * lax.rem(mp, 2)
    over = lax.rem(mp + 2, NMP)
    sib_over = lax.rem(sib + 2, NMP)

    def mp_peer(r):
        return (dp, lax.rem(mp + r, NMP))

    def at(z, h, y):
        return z * 8 + h * 4 + y

    part_peers = []
    for dz_, dh_, dy_ in OFFSETS:
        odd_, high_, yy_ = lax.rem(odd + dz_, 2), lax.rem(high + dh_, 2), lax.rem(yy + dy_, 4)
        part_peers.append(((at(quad * 2 + odd_, high_, yy_), mp), at(odd_, high_, yy_)))

    def quad_peer(k):
        return (at(lax.rem(quad + k, QUADS) * 2 + odd, high, yy), mp)

    wrap = (at(zed, 1 - high, yy), over)

    sent = []

    def remote(src, dst, ss, rs, dev):
        c = pltpu.make_async_remote_copy(
            src_ref=src, dst_ref=dst, send_sem=ss, recv_sem=rs,
            device_id=dev, device_id_type=MESH,
        )
        sent.append(c)
        return c

    barrier = pltpu.get_barrier_semaphore()
    near = [mp_peer(r) for r in (1, 2, 3)] + [wrap]
    near += [(at(zed, high, lax.rem(yy + k, 4)), mp) for k in (1, 3)]
    near += [(at(lax.rem(zed + k, 8), high, yy), mp) for k in (1, 7)]

    def greet(sem):
        for dev in near:
            pl.semaphore_signal(sem, inc=1, device_id=dev, device_id_type=MESH)

    def hear(sem):
        pl.semaphore_wait(sem, len(near))

    greet(barrier)

    loads = []

    def load(src, dst):
        c = pltpu.make_async_copy(src, dst, load_sem.at[len(loads)])
        c.start()
        loads.append(c)
        return c

    l_tok = load(tok_h, tok)
    l_enc = load(enc_h, enc)
    l_head = load(head_h, hd.at[mp])
    l_tin = load(tin_h, tin)
    l_fc1 = [load(fc1_h.at[:, pl.ds(n * 256, 256)], fc1.at[n]) for n in range(4)]
    l_fc2 = [load(fc2_h.at[:, pl.ds(n * 256, 256)], fc2.at[n]) for n in range(4)]

    l_tok.wait()
    l_enc.wait()
    z_s[...] = dot(enc[...], tok[...]).astype(BF16)
    l_head.wait()

    hear(barrier)
    greet(ring.at[0])
    c_z = [
        remote(z_s, z_r.at[r - 1], z_ss.at[r - 1], z_rs.at[r - 1], mp_peer(r)) for r in (2, 1, 3)
    ]
    for c in c_z:
        c.start()
    cuts = (pl.ds(0, 224), pl.ds(224, 224), pl.ds(448, 320))
    c_wrap = []
    for i, dev in enumerate((wrap, wrap, (dp, over))):
        c_wrap.append(
            remote(hd.at[mp, cuts[i]], hd.at[mp, cuts[i]], hd_ss.at[i], hd_rs.at[i], dev)
        )
    for c in c_wrap:
        c.start()
    c_sib = remote(hd.at[mp], hd.at[mp], hd_ss.at[3], hd_rs.at[3], (dp, sib))
    c_sib.start()

    l_tin.wait()
    for n in range(4):
        l_fc1[n].wait()
        th[:, n * 256:(n + 1) * 256] = gelu(dot(tin[...], fc1[n])).astype(BF16)
    l_codes = load(codes_h, codes)
    l_cnt = load(cnt_h, cnt)
    l_sum = load(sum_h, esum)
    l_dec = load(dec_h, dec)

    def rows_of(m):
        return pl.ds(pl.multiple_of(m * OWN, OWN), OWN)

    c_tp = []

    def to_core(cols, m, slot, i):
        c = remote(
            tp.at[cols, rows_of(m)], tp_r.at[slot, cols], tp_ss.at[i], tp_rs.at[i], (dp, sib)
        )
        c.start()
        c_tp.append(c)

    pairs = (pl.ds(0, 2), pl.ds(2, 2))
    for i in range(2):
        for n in (2 * i, 2 * i + 1):
            l_fc2[n].wait()
            tp[n] = dot(th[...], fc2[n]).astype(BF16)
        to_core(pairs[i], sib_over, 0, i)
    to_core(pl.ds(0, 4), sib, 1, 2)

    hear(ring.at[0])
    greet(ring.at[1])

    l_codes.wait()
    code = jnp.broadcast_to(codes[...], (32, ROWS))
    code_hi = jnp.right_shift(code, 7)
    code_lo = jnp.broadcast_to(jnp.bitwise_and(codes[...], 127), (128, ROWS))
    lo_id = lax.broadcasted_iota(jnp.int32, (128, ROWS), 0)
    lo_hot = jnp.where(lo_id == code_lo, 1.0, 0.0).astype(BF16)

    c_chip = []
    for i in range(2):
        c_tp[i].wait_recv()
        for n in (2 * i, 2 * i + 1):
            tp_s[n] = (tp[n, rows_of(over), :].astype(F32) + tp_r[0, n].astype(F32)).astype(BF16)
        c = remote(
            tp_s.at[pairs[i]], tp_r.at[2, pairs[i]], tp_ss.at[3 + i], tp_rs.at[3 + i], (dp, over)
        )
        c.start()
        c_chip.append(c)

    hear(ring.at[1])
    greet(ring.at[2])

    for c in c_z:
        c.wait_recv()
    z_t = z_s[...].astype(F32)
    for r in range(3):
        z_t = z_t + z_r[r].astype(F32)
    hi_id = lax.broadcasted_iota(jnp.int32, (QHI, ROWS), 0) + mp * QHI
    hi_hot = jnp.where(hi_id == code_hi[0:QHI], 1.0, 0.0).astype(BF16)
    counts = dot(hi_hot, lo_hot, 1, 1)
    for i in range(QHI // 2):
        pair = [jnp.where(code_hi == mp * QHI + i * 2 + j, z_t, 0.0) for j in range(2)]
        pair = dot(jnp.concatenate(pair, axis=0).astype(BF16), lo_hot, 1, 1).astype(BF16)
        for j in range(2):
            s_s[i * 2 + j, 0:CD] = pair[j * CD:(j + 1) * CD]
            s_s[i * 2 + j, CD:SROW] = count_rows(counts[i * 2 + j:i * 2 + j + 1])
    hear(ring.at[2])
    greet(ring.at[3])

    def to_parts(src, dst, ss, rs):
        started = []
        for i, (dev, p) in enumerate(part_peers):
            c = remote(src.at[p], dst.at[i], ss.at[i], rs.at[i], dev)
            c.start()
            started.append(c)
        return started

    def to_quads(buf, ss, rs):
        started = []
        for k in (2, 1, 3):
            c = remote(buf.at[quad], buf.at[quad], ss.at[k - 1], rs.at[k - 1], quad_peer(k))
            c.start()
            started.append(c)
        return started

    def from_part(src, dst, ss, rs):
        started = []
        for i, (dev, _) in enumerate(part_peers):
            c = remote(src, dst.at[part], ss.at[i], rs.at[i], dev)
            c.start()
            started.append(c)
        return started

    def arrive(copies):
        for c in copies:
            c.wait_recv()

    z_rows[...] = z_t.T

    l_cnt.wait()
    l_sum.wait()
    l_dec.wait()
    lo_twice = jnp.concatenate([lo_hot, lo_hot], axis=0)
    inv = 1.0 / cnt[...]
    for h in range(HI):
        vector = esum[:, h * 128:(h + 1) * 128] * inv[h:h + 1, :]
        upper = vector.astype(BF16)
        book[h * 32:(h + 1) * 32, 0:128] = upper
        book[h * 32:(h + 1) * 32, 128:256] = (vector - upper.astype(F32)).astype(BF16)
    q_t = jnp.zeros((32, ROWS), F32)
    for i in range(HI // 8):
        found = dot(book[i * 256:(i + 1) * 256, :], lo_twice)
        for j in range(8):
            q_t = q_t + jnp.where(code_hi == i * 8 + j, found[j * 32:(j + 1) * 32], 0.0)
    q_rows[...] = q_t.T
    q_round_t = q_t.astype(BF16)
    own_rows = pl.ds(pl.multiple_of(mp * OWN, OWN), OWN)
    hidden, slope = gelu_and_slope(dot(q_rows[own_rows, :].astype(BF16), dec[...]))
    hidden = hidden.astype(BF16)

    hear(ring.at[3])
    c_s1 = to_parts(s_s, s_r, s1_ss, s1_rs)

    c_sib.wait_recv()
    c_fwd = []
    for i in range(3):
        c_wrap[i].wait_recv()
        rows = hd.at[over, cuts[i]]
        c = remote(rows, rows, hd_ss.at[4 + i], hd_rs.at[4 + i], (dp, sib))
        c.start()
        c_fwd.append(c)
    for b in (mp, sib, over):
        pred[b] = dot(hidden, hd[b])
    for c in c_fwd:
        c.wait_recv()
    pred[sib_over] = dot(hidden, hd[sib_over])

    arrive([c_tp[2]] + c_chip)
    target = []
    for n in range(4):
        t = tin[own_rows, n * 256:(n + 1) * 256].astype(F32) + tp[n, own_rows, :].astype(F32)
        t = t + tp_r[1, n].astype(F32) + tp_r[2, n].astype(F32)
        target.append(t)
    pp = jnp.zeros((OWN, 256), F32)
    pt = jnp.zeros((OWN, 256), F32)
    tt = jnp.zeros((OWN, 256), F32)
    for n in range(4):
        pp = pp + pred[n] * pred[n]
        pt = pt + pred[n] * target[n]
        tt = tt + target[n] * target[n]
    pp = jnp.sum(pp, axis=1, keepdims=True) + EPS
    pt = jnp.sum(pt, axis=1, keepdims=True)
    tt = jnp.sum(tt, axis=1, keepdims=True) + EPS
    inverse = 1.0 / (jnp.sqrt(pp) * jnp.sqrt(tt))
    scale = pt * inverse / pp
    for n in range(4):
        dp_s[n] = (scale * pred[n] - inverse * target[n]).astype(BF16)
    c_dp = []
    for r in (2, 1, 3):
        c = remote(
            dp_s.at[lax.rem(mp + r, NMP)], dp_r.at[mp], dp_ss.at[r - 1], dp_rs.at[r - 1],
            mp_peer(r),
        )
        c.start()
        c_dp.append(c)
    dp_r[mp] = dp_s[mp]
    dh = dot(dp_s[0], hd[0], 1, 1)
    for n in range(1, 4):
        dh = dh + dot(dp_s[n], hd[n], 1, 1)
    dpre = (dh * slope).astype(BF16)

    q_own = q_rows[own_rows, :]
    gd[mp] = dot(q_own.T.astype(BF16), dpre).astype(BF16)
    dq = dot(dpre, dec[...], 1, 1)
    dz[mp] = (dq + 2.0 * BETA * (z_rows[own_rows, :] - q_own)).astype(BF16)
    c_small = []
    for r in (2, 1, 3):
        for buf, ss, rs in ((gd, gd_ss, gd_rs), (dz, dz_ss, dz_rs)):
            c = remote(buf.at[mp], buf.at[mp], ss.at[r - 1], rs.at[r - 1], mp_peer(r))
            c.start()
            c_small.append(c)

    arrive(c_s1)
    sums, counts = add_sums([s_s[part]] + [s_r[i] for i in range(PARTS - 1)])
    s_z[quad, 0:CD] = sums
    s_z[quad, CD:SROW] = counts
    c_s2 = to_quads(s_z, s2_ss, s2_rs)

    dec_t = dec[...].astype(F32).T.astype(BF16)
    for n in range(3):
        hid_t[n * 256:(n + 1) * 256, :] = gelu(
            dot(dec_t[n * 256:(n + 1) * 256], q_round_t)
        ).astype(BF16)

    arrive(c_dp)
    grad = dot(hid_t[...], dp_r[...].reshape(ROWS, 256)).astype(BF16)
    for i in range(PARTS):
        g_s[i] = grad[i * GROW:(i + 1) * GROW]
    c_g1 = to_parts(g_s, g_r, g1_ss, g1_rs)

    arrive(c_small)
    grad_dec = add_up([gd[m] for m in range(NMP)]).astype(BF16)
    dz_t = dz[...].reshape(ROWS, CD).astype(F32).T.astype(BF16)
    grad_enc = dot(dz_t, tok[...], 1, 1).astype(BF16)
    for n in range(6):
        for i in range(2):
            x_s[n * 2 + i] = grad_dec[i * 16:(i + 1) * 16, n * 128:(n + 1) * 128]
    for i in range(2):
        x_s[12 + i] = grad_enc[i * 16:(i + 1) * 16, 0:128]
        x_s[14 + i, :, 0:64] = grad_enc[i * 16:(i + 1) * 16, 128:192]
        x_s[14 + i, :, 64:128] = jnp.zeros((XROW, 64), BF16)
    c_x1 = to_parts(x_s, x_r, x1_ss, x1_rs)

    arrive(c_s2)
    sums, counts = add_sums([s_z[k] for k in range(QUADS)])
    s_all[mp, part, 0:CD] = sums
    s_all[mp, part, CD:SROW] = counts
    c_s3 = from_part(s_all.at[mp, part], s_all.at[mp], s3_ss, s3_rs)

    arrive(c_g1)
    g_z[quad] = add_up([g_s[part]] + [g_r[i] for i in range(PARTS - 1)]).astype(BF16)
    c_g2 = to_quads(g_z, g2_ss, g2_rs)
    arrive(c_x1)
    x_z[quad] = add_up([x_s[part]] + [x_r[i] for i in range(PARTS - 1)]).astype(BF16)
    c_x2 = to_quads(x_z, x2_ss, x2_rs)

    arrive(c_s3)
    halves = (pl.ds(0, PARTS // 2), pl.ds(PARTS // 2, PARTS // 2))
    c_over = []
    for i, dev in enumerate(((dp, over), wrap)):
        rows = s_all.at[mp, halves[i]]
        c = remote(rows, rows, s4_ss.at[i], s4_rs.at[i], dev)
        c.start()
        c_over.append(c)
    c_near = remote(s_all.at[mp], s_all.at[mp], s4_ss.at[2], s4_rs.at[2], (dp, sib))
    c_near.start()

    outs = []

    def store(src, dst):
        c = pltpu.make_async_copy(src, dst, out_sem.at[len(outs)])
        c.start()
        outs.append(c)

    arrive(c_g2)
    g_sum[...] = add_up([g_z[k] for k in range(QUADS)]).astype(BF16)
    c_g3 = from_part(g_sum, grads_h, g3_ss, g3_rs)
    store(g_sum, grads_h.at[part])
    arrive(c_x2)
    x_sum[...] = add_up([x_z[k] for k in range(QUADS)]).astype(BF16)
    c_x3 = from_part(x_sum, small_h, x3_ss, x3_rs)
    store(x_sum, small_h.at[part])

    c_last = []
    for i in range(2):
        c_over[i].wait_recv()
        rows = s_all.at[over, halves[i]]
        c = remote(rows, rows, s4_ss.at[3 + i], s4_rs.at[3 + i], (dp, sib))
        c.start()
        c_last.append(c)

    arrive(c_last + [c_near])
    for m in range(NMP):
        for i in range(QHI):
            h = m * QHI + i
            columns = slice(h * 128, (h + 1) * 128)
            o_sum[:, columns] = DECAY * esum[:, columns] + (1.0 - DECAY) * s_all[
                m, i, 0:CD
            ].astype(F32)
            rows = s_all[m, i, CD:SROW].astype(F32)
            o_count[h:h + 1] = DECAY * cnt[h:h + 1] + (1.0 - DECAY) * (rows[0:1] + rows[1:2])
    store(o_count, ncount_h)
    store(o_sum, nsum_h)

    arrive(c_g3)
    arrive(c_x3)
    for c in sent:
        c.wait_send()
    for c in outs:
        c.wait()


def results(
    count_h, sum_h, grads_h, small_h, ncount_h, nsum_h, ghead_h, gdec_h, genc_h,
    count, sums, grads, small, head, dec, enc, in_sem, out_sem,
):
    parts = [pl.ds(i * 4, 4) for i in range(PARTS // 4)]
    columns = [pl.ds(i * 2048, 2048) for i in range(4)]
    ins = [(grads_h.at[p], grads.at[p]) for p in parts] + [(small_h, small)]
    ins += [(sum_h.at[:, c], sums.at[:, c]) for c in columns] + [(count_h, count)]
    ins = [pltpu.make_async_copy(*pair, in_sem.at[i]) for i, pair in enumerate(ins)]
    for c in ins:
        c.start()
    outs = []

    def store(src, dst):
        c = pltpu.make_async_copy(src, dst, out_sem.at[len(outs)])
        c.start()
        outs.append(c)

    for i, p in enumerate(parts):
        ins[i].wait()
        head[p] = grads[p].astype(F32)
        store(head.at[p], ghead_h.at[p])
    ins[4].wait()
    for n in range(6):
        for i in range(2):
            dec[i * 16:(i + 1) * 16, n * 128:(n + 1) * 128] = small[n * 2 + i].astype(F32)
    store(dec, gdec_h)
    for i in range(2):
        enc[i * 16:(i + 1) * 16, 0:128] = small[12 + i].astype(F32)
        enc[i * 16:(i + 1) * 16, 128:192] = small[14 + i, :, 0:64].astype(F32)
    store(enc, genc_h)
    for i, c in enumerate(columns):
        ins[5 + i].wait()
        store(sums.at[:, c], nsum_h.at[:, c])
    ins[9].wait()
    store(count, ncount_h)
    for c in outs:
        c.wait()


def on_device(
    teacher_in, teacher_fc1, teacher_fc2, tok_in, enc_proj, codes, ema_count, ema_sum, dec_in, head
):
    def sems(*shape):
        return pltpu.SemaphoreType.DMA(shape)

    def two(*shape):
        return [sems(*shape), sems(*shape)]

    vm = pltpu.VMEM
    local = [
        vm((ROWS, 1024), BF16), vm((4, 1024, 256), BF16), vm((4, 1024, 256), BF16),
        vm((192, ROWS), BF16), vm((CD, 192), BF16), vm((1, ROWS), jnp.int32),
        vm((HI, 128), F32), vm((CD, 8192), F32), vm((CD, 768), BF16),
        vm((ROWS, 1024), BF16), vm((4, ROWS, 256), BF16), vm((768, ROWS), BF16),
        vm((ROWS, CD), F32), vm((ROWS, CD), F32), vm((HI * CD, 256), BF16),
        vm((4, OWN, 256), F32),
    ]
    exchanged = [
        vm((4, 768, 256), BF16), vm((4, OWN, 256), BF16), vm((3, 4, OWN, 256), BF16),
        vm((CD, ROWS), BF16),
        vm((3, CD, ROWS), BF16),
        vm((PARTS, SROW, 128), BF16), vm((PARTS - 1, SROW, 128), BF16),
        vm((QUADS, SROW, 128), BF16), vm((NMP, PARTS, SROW, 128), BF16),
        vm((4, OWN, 256), BF16), vm((4, OWN, 256), BF16),
        vm((NMP, CD, 768), BF16), vm((NMP, OWN, CD), BF16),
        vm((PARTS, GROW, 256), BF16), vm((PARTS - 1, GROW, 256), BF16),
        vm((QUADS, GROW, 256), BF16), vm((GROW, 256), BF16),
        vm((PARTS, XROW, 128), BF16), vm((PARTS - 1, XROW, 128), BF16),
        vm((QUADS, XROW, 128), BF16), vm((XROW, 128), BF16),
    ]
    made = [vm((HI, 128), F32), vm((CD, 8192), F32)]
    semaphores = [pltpu.SemaphoreType.REGULAR((4,)), sems(16), sems(4)]
    semaphores += two(7) + two(5) + two(3) + two(15) + two(3) + two(15)
    semaphores += two(5) + two(3) + two(3) + two(3) + two(15) + two(3)
    semaphores += two(15) + two(15) + two(3) + two(15)
    anywhere = pl.BlockSpec(memory_space=pl.ANY)
    outs = pl.pallas_call(
        kernel,
        out_shape=(
            jax.ShapeDtypeStruct((HI, 128), F32),
            jax.ShapeDtypeStruct((32, 8192), F32),
            jax.ShapeDtypeStruct((PARTS, GROW, 256), BF16),
            jax.ShapeDtypeStruct((PARTS, XROW, 128), BF16),
        ),
        in_specs=[pl.BlockSpec(memory_space=pltpu.HBM)] * 10,
        out_specs=(anywhere,) * 4,
        scratch_shapes=local + exchanged + made + semaphores,
        compiler_params=pltpu.CompilerParams(
            collective_id=0, has_side_effects=True, vmem_limit_bytes=64 * 2**20
        ),
        name="step",
    )(
        teacher_in, teacher_fc1, teacher_fc2, tok_in.T, enc_proj.T, codes.reshape(1, ROWS),
        ema_count.reshape(HI, 128), ema_sum, dec_in, head,
    )
    final = [(HI, 128), (CD, 8192), (PARTS, GROW, 256), (CD, 768), (CD, 192)]
    outs = pl.pallas_call(
        results,
        out_shape=tuple(jax.ShapeDtypeStruct(shape, F32) for shape in final),
        in_specs=[pl.BlockSpec(memory_space=pltpu.HBM)] * 4,
        out_specs=(pl.BlockSpec(memory_space=pltpu.HBM),) * 5,
        scratch_shapes=[vm(final[0], F32), vm(final[1], F32)]
        + [vm((PARTS, GROW, 256), BF16), vm((PARTS, XROW, 128), BF16)]
        + [vm(shape, F32) for shape in final[2:]]
        + [sems(10), sems(11)],
        compiler_params=pltpu.CompilerParams(vmem_limit_bytes=64 * 2**20),
        name="results",
    )(*outs)
    return (outs[0].reshape(8192), outs[1], outs[2].reshape(768, 256), outs[3], outs[4].T)


def solution(mesh):
    placed = (
        P("dp", None),
        P(None, "mp"),
        P("mp", None),
        P("dp", "mp"),
        P("mp", None),
        P("dp"),
        P(),
        P(),
        P(),
        P(None, "mp"),
    )
    return jax.shard_map(
        on_device,
        mesh=mesh,
        in_specs=placed,
        out_specs=(P(), P(), P(None, "mp"), P(), P("mp", None)),
        check_vma=False,
    )
```

```python
import functools
import math

import jax
import jax.numpy as jnp
from jax import lax
from jax.experimental import pallas as pl
from jax.experimental.pallas import tpu as pltpu
from jax.sharding import PartitionSpec as P

DECAY = 0.5
BETA = 0.25
EPS = 1e-06
MESH = pl.DeviceIdType.MESH
F32 = jnp.float32
BF16 = jnp.bfloat16
GELU_A = math.sqrt(2.0 / math.pi)
GELU_B = 0.044715

NMP = 4
PARTS = 16
QUADS = 4
ROWS = 256
OWN = 64
HI = 64
QHI = 16
CD = 32
SROW = 48
GROW = 48
XROW = 16
OFFSETS = sorted(
    [(z, h, y) for z in range(2) for h in range(2) for y in range(4) if z + h + y > 0],
    key=lambda o: -(o[0] + 2 * o[1] + min(o[2], 4 - o[2])),
)

def gelu(x):
    return 0.5 * x * (1.0 + jnp.tanh(GELU_A * (x + GELU_B * (x * x * x))))


def gelu_and_slope(x):
    square = x * x
    t = jnp.tanh(GELU_A * (x + GELU_B * (square * x)))
    value = 0.5 * x * (1.0 + t)
    slope = 0.5 * (1.0 + t) + (0.5 * GELU_A) * x * (1.0 - t * t) * (
        1.0 + (3.0 * GELU_B) * square
    )
    return value, slope


def count_rows(counts):
    upper = counts.astype(BF16).astype(F32)
    row = lax.broadcasted_iota(jnp.int32, (SROW - CD, 128), 0)
    rest = jnp.where(row == 1, counts - upper, 0.0)
    return jnp.where(row == 0, upper, rest).astype(BF16)


def add_up(parts):
    total = parts[0].astype(F32)
    for part in parts[1:]:
        total = total + part.astype(F32)
    return total


def add_sums(parts):
    total = add_up(parts)
    counts = total[CD:CD + 1] + total[CD + 1:CD + 2]
    return total[0:CD].astype(BF16), count_rows(counts)


def dot(a, b, ca=1, cb=0):
    return lax.dot_general(a, b, (((ca,), (cb,)), ((), ())), preferred_element_type=F32)


def kernel(
    tin_h, fc1_h, fc2_h, tok_h, enc_h, codes_h, cnt_h, sum_h, dec_h, head_h,
    ncount_h, nsum_h, grads_h, small_h,
    tin, fc1, fc2, tok, enc, codes, cnt, esum, dec,
    th, tp, hid_t, q_rows, z_rows, book, pred,
    hd, tp_s, tp_r, z_s, z_r, s_s, s_r, s_z, s_all, dp_s, dp_r, gd, dz,
    g_s, g_r, g_z, g_sum, x_s, x_r, x_z, x_sum,
    o_count, o_sum,
    ring, load_sem, out_sem,
    hd_ss, hd_rs, tp_ss, tp_rs, z_ss, z_rs, s1_ss, s1_rs, s2_ss, s2_rs, s3_ss, s3_rs,
    s4_ss, s4_rs, dp_ss, dp_rs, gd_ss, gd_rs, dz_ss, dz_rs, g1_ss, g1_rs, g2_ss, g2_rs,
    g3_ss, g3_rs, x1_ss, x1_rs, x2_ss, x2_rs, x3_ss, x3_rs,
):
    dp = lax.axis_index("dp")
    mp = lax.axis_index("mp")
    zed = lax.div(dp, 8)
    high = lax.rem(lax.div(dp, 4), 2)
    yy = lax.rem(dp, 4)
    odd = lax.rem(zed, 2)
    quad = lax.div(zed, 2)
    part = odd * 8 + high * 4 + yy
    sib = mp + 1 - 2 * lax.rem(mp, 2)
    over = lax.rem(mp + 2, NMP)
    sib_over = lax.rem(sib + 2, NMP)

    def mp_peer(r):
        return (dp, lax.rem(mp + r, NMP))

    def at(z, h, y):
        return z * 8 + h * 4 + y

    part_peers = []
    for dz_, dh_, dy_ in OFFSETS:
        odd_, high_, yy_ = lax.rem(odd + dz_, 2), lax.rem(high + dh_, 2), lax.rem(yy + dy_, 4)
        part_peers.append(((at(quad * 2 + odd_, high_, yy_), mp), at(odd_, high_, yy_)))

    def quad_peer(k):
        return (at(lax.rem(quad + k, QUADS) * 2 + odd, high, yy), mp)

    wrap = (at(zed, 1 - high, yy), over)

    sent = []

    def remote(src, dst, ss, rs, dev):
        c = pltpu.make_async_remote_copy(
            src_ref=src, dst_ref=dst, send_sem=ss, recv_sem=rs,
            device_id=dev, device_id_type=MESH,
        )
        sent.append(c)
        return c

    barrier = pltpu.get_barrier_semaphore()
    near = [mp_peer(r) for r in (1, 2, 3)] + [wrap]
    near += [(at(zed, high, lax.rem(yy + k, 4)), mp) for k in (1, 3)]
    near += [(at(lax.rem(zed + k, 8), high, yy), mp) for k in (1, 7)]

    ahead = [near[1]] + near[3:]

    def greet(sem, devices=ahead):
        for dev in devices:
            pl.semaphore_signal(sem, inc=1, device_id=dev, device_id_type=MESH)

    def hear(sem, devices=ahead):
        pl.semaphore_wait(sem, len(devices))

    greet(barrier, near)

    loads = []

    def load(src, dst):
        c = pltpu.make_async_copy(src, dst, load_sem.at[len(loads)])
        c.start()
        loads.append(c)
        return c

    l_tok = load(tok_h, tok)
    l_enc = load(enc_h, enc)
    l_head = load(head_h, hd.at[mp])
    l_tin = load(tin_h, tin)
    l_fc1 = [load(fc1_h.at[:, pl.ds(n * 256, 256)], fc1.at[n]) for n in range(4)]
    l_fc2 = [load(fc2_h.at[:, pl.ds(n * 256, 256)], fc2.at[n]) for n in range(4)]

    l_tok.wait()
    l_enc.wait()
    z_s[...] = dot(enc[...], tok[...]).astype(BF16)
    l_head.wait()

    hear(barrier, near)
    greet(ring.at[0])
    c_z = [
        remote(z_s, z_r.at[r - 1], z_ss.at[r - 1], z_rs.at[r - 1], mp_peer(r)) for r in (2, 1, 3)
    ]
    for c in c_z:
        c.start()
    cuts = (pl.ds(0, 224), pl.ds(224, 224), pl.ds(448, 320))
    c_wrap = []
    for i, dev in enumerate((wrap, wrap, (dp, over))):
        c_wrap.append(
            remote(hd.at[mp, cuts[i]], hd.at[mp, cuts[i]], hd_ss.at[i], hd_rs.at[i], dev)
        )
    for c in c_wrap:
        c.start()
    c_sib = remote(hd.at[mp], hd.at[mp], hd_ss.at[3], hd_rs.at[3], (dp, sib))
    c_sib.start()

    l_tin.wait()
    for n in range(4):
        l_fc1[n].wait()
        th[:, n * 256:(n + 1) * 256] = gelu(dot(tin[...], fc1[n])).astype(BF16)
    l_codes = load(codes_h, codes)
    l_cnt = load(cnt_h, cnt)
    l_sum = load(sum_h, esum)
    l_dec = load(dec_h, dec)

    def rows_of(m):
        return pl.ds(pl.multiple_of(m * OWN, OWN), OWN)

    c_tp = []

    def to_core(cols, m, slot, i):
        c = remote(
            tp.at[cols, rows_of(m)], tp_r.at[slot, cols], tp_ss.at[i], tp_rs.at[i], (dp, sib)
        )
        c.start()
        c_tp.append(c)

    pairs = (pl.ds(0, 2), pl.ds(2, 2))
    for i in range(2):
        for n in (2 * i, 2 * i + 1):
            l_fc2[n].wait()
            tp[n] = dot(th[...], fc2[n]).astype(BF16)
        to_core(pairs[i], sib_over, 0, i)
    to_core(pl.ds(0, 4), sib, 1, 2)

    hear(ring.at[0])
    greet(ring.at[1])

    l_codes.wait()
    code = jnp.broadcast_to(codes[...], (32, ROWS))
    code_hi = jnp.right_shift(code, 7)
    code_lo = jnp.broadcast_to(jnp.bitwise_and(codes[...], 127), (128, ROWS))
    lo_id = lax.broadcasted_iota(jnp.int32, (128, ROWS), 0)
    lo_hot = jnp.where(lo_id == code_lo, 1.0, 0.0).astype(BF16)

    c_chip = []
    for i in range(2):
        c_tp[i].wait_recv()
        for n in (2 * i, 2 * i + 1):
            tp_s[n] = (tp[n, rows_of(over), :].astype(F32) + tp_r[0, n].astype(F32)).astype(BF16)
        c = remote(
            tp_s.at[pairs[i]], tp_r.at[2, pairs[i]], tp_ss.at[3 + i], tp_rs.at[3 + i], (dp, over)
        )
        c.start()
        c_chip.append(c)

    hear(ring.at[1])
    greet(ring.at[2])

    for c in c_z:
        c.wait_recv()
    z_t = z_s[...].astype(F32)
    for r in range(3):
        z_t = z_t + z_r[r].astype(F32)
    hi_id = lax.broadcasted_iota(jnp.int32, (QHI, ROWS), 0) + mp * QHI
    hi_hot = jnp.where(hi_id == code_hi[0:QHI], 1.0, 0.0).astype(BF16)
    counts = dot(hi_hot, lo_hot, 1, 1)
    for i in range(QHI // 2):
        pair = [jnp.where(code_hi == mp * QHI + i * 2 + j, z_t, 0.0) for j in range(2)]
        pair = dot(jnp.concatenate(pair, axis=0).astype(BF16), lo_hot, 1, 1).astype(BF16)
        for j in range(2):
            s_s[i * 2 + j, 0:CD] = pair[j * CD:(j + 1) * CD]
            s_s[i * 2 + j, CD:SROW] = count_rows(counts[i * 2 + j:i * 2 + j + 1])
    hear(ring.at[2])
    greet(ring.at[3])

    def to_parts(src, dst, ss, rs):
        started = []
        for i, (dev, p) in enumerate(part_peers):
            c = remote(src.at[p], dst.at[i], ss.at[i], rs.at[i], dev)
            c.start()
            started.append(c)
        return started

    def to_quads(buf, ss, rs):
        started = []
        for k in (2, 1, 3):
            c = remote(buf.at[quad], buf.at[quad], ss.at[k - 1], rs.at[k - 1], quad_peer(k))
            c.start()
            started.append(c)
        return started

    def from_part(src, dst, ss, rs):
        started = []
        for i, (dev, _) in enumerate(part_peers):
            c = remote(src, dst.at[part], ss.at[i], rs.at[i], dev)
            c.start()
            started.append(c)
        return started

    def arrive(copies):
        for c in copies:
            c.wait_recv()

    z_rows[...] = z_t.T

    l_cnt.wait()
    l_sum.wait()
    l_dec.wait()
    lo_twice = jnp.concatenate([lo_hot, lo_hot], axis=0)
    inv = 1.0 / cnt[...]
    for h in range(HI):
        vector = esum[:, h * 128:(h + 1) * 128] * inv[h:h + 1, :]
        upper = vector.astype(BF16)
        book[h * 32:(h + 1) * 32, 0:128] = upper
        book[h * 32:(h + 1) * 32, 128:256] = (vector - upper.astype(F32)).astype(BF16)
    q_t = jnp.zeros((32, ROWS), F32)
    for i in range(HI // 8):
        found = dot(book[i * 256:(i + 1) * 256, :], lo_twice)
        for j in range(8):
            q_t = q_t + jnp.where(code_hi == i * 8 + j, found[j * 32:(j + 1) * 32], 0.0)
    q_rows[...] = q_t.T
    q_round_t = q_t.astype(BF16)
    own_rows = pl.ds(pl.multiple_of(mp * OWN, OWN), OWN)
    hidden, slope = gelu_and_slope(dot(q_rows[own_rows, :].astype(BF16), dec[...]))
    hidden = hidden.astype(BF16)

    hear(ring.at[3])
    c_s1 = to_parts(s_s, s_r, s1_ss, s1_rs)

    c_sib.wait_recv()
    c_fwd = []
    for i in range(3):
        c_wrap[i].wait_recv()
        rows = hd.at[over, cuts[i]]
        c = remote(rows, rows, hd_ss.at[4 + i], hd_rs.at[4 + i], (dp, sib))
        c.start()
        c_fwd.append(c)
    for b in (mp, sib, over):
        pred[b] = dot(hidden, hd[b])
    for c in c_fwd:
        c.wait_recv()
    pred[sib_over] = dot(hidden, hd[sib_over])

    arrive([c_tp[2]] + c_chip)
    target = []
    for n in range(4):
        t = tin[own_rows, n * 256:(n + 1) * 256].astype(F32) + tp[n, own_rows, :].astype(F32)
        t = t + tp_r[1, n].astype(F32) + tp_r[2, n].astype(F32)
        target.append(t)
    pp = jnp.zeros((OWN, 256), F32)
    pt = jnp.zeros((OWN, 256), F32)
    tt = jnp.zeros((OWN, 256), F32)
    for n in range(4):
        pp = pp + pred[n] * pred[n]
        pt = pt + pred[n] * target[n]
        tt = tt + target[n] * target[n]
    pp = jnp.sum(pp, axis=1, keepdims=True) + EPS
    pt = jnp.sum(pt, axis=1, keepdims=True)
    tt = jnp.sum(tt, axis=1, keepdims=True) + EPS
    inverse = 1.0 / (jnp.sqrt(pp) * jnp.sqrt(tt))
    scale = pt * inverse / pp
    for n in range(4):
        dp_s[n] = (scale * pred[n] - inverse * target[n]).astype(BF16)
    c_dp = []
    for r in (2, 1, 3):
        c = remote(
            dp_s.at[lax.rem(mp + r, NMP)], dp_r.at[mp], dp_ss.at[r - 1], dp_rs.at[r - 1],
            mp_peer(r),
        )
        c.start()
        c_dp.append(c)
    dp_r[mp] = dp_s[mp]
    dh = dot(dp_s[0], hd[0], 1, 1)
    for n in range(1, 4):
        dh = dh + dot(dp_s[n], hd[n], 1, 1)
    dpre = (dh * slope).astype(BF16)

    q_own = q_rows[own_rows, :]
    gd[mp] = dot(q_own.T.astype(BF16), dpre).astype(BF16)
    dq = dot(dpre, dec[...], 1, 1)
    dz[mp] = (dq + 2.0 * BETA * (z_rows[own_rows, :] - q_own)).astype(BF16)
    c_small = []
    for r in (2, 1, 3):
        for buf, ss, rs in ((gd, gd_ss, gd_rs), (dz, dz_ss, dz_rs)):
            c = remote(buf.at[mp], buf.at[mp], ss.at[r - 1], rs.at[r - 1], mp_peer(r))
            c.start()
            c_small.append(c)

    arrive(c_s1)
    sums, counts = add_sums([s_s[part]] + [s_r[i] for i in range(PARTS - 1)])
    s_z[quad, 0:CD] = sums
    s_z[quad, CD:SROW] = counts
    c_s2 = to_quads(s_z, s2_ss, s2_rs)

    dec_t = dec[...].astype(F32).T.astype(BF16)
    for n in range(3):
        hid_t[n * 256:(n + 1) * 256, :] = gelu(
            dot(dec_t[n * 256:(n + 1) * 256], q_round_t)
        ).astype(BF16)

    arrive(c_dp)
    grad = dot(hid_t[...], dp_r[...].reshape(ROWS, 256)).astype(BF16)
    for i in range(PARTS):
        g_s[i] = grad[i * GROW:(i + 1) * GROW]
    c_g1 = to_parts(g_s, g_r, g1_ss, g1_rs)

    arrive(c_small)
    grad_dec = add_up([gd[m] for m in range(NMP)]).astype(BF16)
    dz_t = dz[...].reshape(ROWS, CD).astype(F32).T.astype(BF16)
    grad_enc = dot(dz_t, tok[...], 1, 1).astype(BF16)
    for n in range(6):
        for i in range(2):
            x_s[n * 2 + i] = grad_dec[i * 16:(i + 1) * 16, n * 128:(n + 1) * 128]
    for i in range(2):
        x_s[12 + i] = grad_enc[i * 16:(i + 1) * 16, 0:128]
        x_s[14 + i, :, 0:64] = grad_enc[i * 16:(i + 1) * 16, 128:192]
        x_s[14 + i, :, 64:128] = jnp.zeros((XROW, 64), BF16)
    c_x1 = to_parts(x_s, x_r, x1_ss, x1_rs)

    arrive(c_s2)
    sums, counts = add_sums([s_z[k] for k in range(QUADS)])
    s_all[mp, part, 0:CD] = sums
    s_all[mp, part, CD:SROW] = counts
    c_s3 = from_part(s_all.at[mp, part], s_all.at[mp], s3_ss, s3_rs)

    arrive(c_g1)
    g_z[quad] = add_up([g_s[part]] + [g_r[i] for i in range(PARTS - 1)]).astype(BF16)
    c_g2 = to_quads(g_z, g2_ss, g2_rs)
    arrive(c_x1)
    x_z[quad] = add_up([x_s[part]] + [x_r[i] for i in range(PARTS - 1)]).astype(BF16)
    c_x2 = to_quads(x_z, x2_ss, x2_rs)

    arrive(c_s3)
    halves = (pl.ds(0, PARTS // 2), pl.ds(PARTS // 2, PARTS // 2))
    c_over = []
    for i, dev in enumerate(((dp, over), wrap)):
        rows = s_all.at[mp, halves[i]]
        c = remote(rows, rows, s4_ss.at[i], s4_rs.at[i], dev)
        c.start()
        c_over.append(c)
    c_near = remote(s_all.at[mp], s_all.at[mp], s4_ss.at[2], s4_rs.at[2], (dp, sib))
    c_near.start()

    outs = []

    def store(src, dst):
        c = pltpu.make_async_copy(src, dst, out_sem.at[len(outs)])
        c.start()
        outs.append(c)

    arrive(c_g2)
    g_sum[...] = add_up([g_z[k] for k in range(QUADS)]).astype(BF16)
    c_g3 = from_part(g_sum, grads_h, g3_ss, g3_rs)
    store(g_sum, grads_h.at[part])
    arrive(c_x2)
    x_sum[...] = add_up([x_z[k] for k in range(QUADS)]).astype(BF16)
    c_x3 = from_part(x_sum, small_h, x3_ss, x3_rs)
    store(x_sum, small_h.at[part])

    c_last = []
    for i in range(2):
        c_over[i].wait_recv()
        rows = s_all.at[over, halves[i]]
        c = remote(rows, rows, s4_ss.at[3 + i], s4_rs.at[3 + i], (dp, sib))
        c.start()
        c_last.append(c)

    arrive(c_last + [c_near])
    for m in range(NMP):
        for i in range(QHI):
            h = m * QHI + i
            columns = slice(h * 128, (h + 1) * 128)
            o_sum[:, columns] = DECAY * esum[:, columns] + (1.0 - DECAY) * s_all[
                m, i, 0:CD
            ].astype(F32)
            rows = s_all[m, i, CD:SROW].astype(F32)
            o_count[h:h + 1] = DECAY * cnt[h:h + 1] + (1.0 - DECAY) * (rows[0:1] + rows[1:2])
    store(o_count, ncount_h)
    store(o_sum, nsum_h)

    arrive(c_g3)
    arrive(c_x3)
    for c in sent:
        c.wait_send()
    for c in outs:
        c.wait()


def results(
    count_h, sum_h, grads_h, small_h, ncount_h, nsum_h, ghead_h, gdec_h, genc_h,
    count, sums, grads, small, head, dec, enc, in_sem, out_sem,
):
    parts = [pl.ds(i * 4, 4) for i in range(PARTS // 4)]
    columns = [pl.ds(i * 2048, 2048) for i in range(4)]
    ins = [(grads_h.at[p], grads.at[p]) for p in parts] + [(small_h, small)]
    ins += [(sum_h.at[:, c], sums.at[:, c]) for c in columns] + [(count_h, count)]
    ins = [pltpu.make_async_copy(*pair, in_sem.at[i]) for i, pair in enumerate(ins)]
    for c in ins:
        c.start()
    outs = []

    def store(src, dst):
        c = pltpu.make_async_copy(src, dst, out_sem.at[len(outs)])
        c.start()
        outs.append(c)

    for i, p in enumerate(parts):
        ins[i].wait()
        head[p] = grads[p].astype(F32)
        store(head.at[p], ghead_h.at[p])
    ins[4].wait()
    for n in range(6):
        for i in range(2):
            dec[i * 16:(i + 1) * 16, n * 128:(n + 1) * 128] = small[n * 2 + i].astype(F32)
    store(dec, gdec_h)
    for i in range(2):
        enc[i * 16:(i + 1) * 16, 0:128] = small[12 + i].astype(F32)
        enc[i * 16:(i + 1) * 16, 128:192] = small[14 + i, :, 0:64].astype(F32)
    store(enc, genc_h)
    for i, c in enumerate(columns):
        ins[5 + i].wait()
        store(sums.at[:, c], nsum_h.at[:, c])
    ins[9].wait()
    store(count, ncount_h)
    for c in outs:
        c.wait()


def on_device(
    teacher_in, teacher_fc1, teacher_fc2, tok_in, enc_proj, codes, ema_count, ema_sum, dec_in, head
):
    def sems(*shape):
        return pltpu.SemaphoreType.DMA(shape)

    def two(*shape):
        return [sems(*shape), sems(*shape)]

    vm = pltpu.VMEM
    local = [
        vm((ROWS, 1024), BF16), vm((4, 1024, 256), BF16), vm((4, 1024, 256), BF16),
        vm((192, ROWS), BF16), vm((CD, 192), BF16), vm((1, ROWS), jnp.int32),
        vm((HI, 128), F32), vm((CD, 8192), F32), vm((CD, 768), BF16),
        vm((ROWS, 1024), BF16), vm((4, ROWS, 256), BF16), vm((768, ROWS), BF16),
        vm((ROWS, CD), F32), vm((ROWS, CD), F32), vm((HI * CD, 256), BF16),
        vm((4, OWN, 256), F32),
    ]
    exchanged = [
        vm((4, 768, 256), BF16), vm((4, OWN, 256), BF16), vm((3, 4, OWN, 256), BF16),
        vm((CD, ROWS), BF16),
        vm((3, CD, ROWS), BF16),
        vm((PARTS, SROW, 128), BF16), vm((PARTS - 1, SROW, 128), BF16),
        vm((QUADS, SROW, 128), BF16), vm((NMP, PARTS, SROW, 128), BF16),
        vm((4, OWN, 256), BF16), vm((4, OWN, 256), BF16),
        vm((NMP, CD, 768), BF16), vm((NMP, OWN, CD), BF16),
        vm((PARTS, GROW, 256), BF16), vm((PARTS - 1, GROW, 256), BF16),
        vm((QUADS, GROW, 256), BF16), vm((GROW, 256), BF16),
        vm((PARTS, XROW, 128), BF16), vm((PARTS - 1, XROW, 128), BF16),
        vm((QUADS, XROW, 128), BF16), vm((XROW, 128), BF16),
    ]
    made = [vm((HI, 128), F32), vm((CD, 8192), F32)]
    semaphores = [pltpu.SemaphoreType.REGULAR((4,)), sems(16), sems(4)]
    semaphores += two(7) + two(5) + two(3) + two(15) + two(3) + two(15)
    semaphores += two(5) + two(3) + two(3) + two(3) + two(15) + two(3)
    semaphores += two(15) + two(15) + two(3) + two(15)
    anywhere = pl.BlockSpec(memory_space=pl.ANY)
    outs = pl.pallas_call(
        kernel,
        out_shape=(
            jax.ShapeDtypeStruct((HI, 128), F32),
            jax.ShapeDtypeStruct((32, 8192), F32),
            jax.ShapeDtypeStruct((PARTS, GROW, 256), BF16),
            jax.ShapeDtypeStruct((PARTS, XROW, 128), BF16),
        ),
        in_specs=[pl.BlockSpec(memory_space=pltpu.HBM)] * 10,
        out_specs=(anywhere,) * 4,
        scratch_shapes=local + exchanged + made + semaphores,
        compiler_params=pltpu.CompilerParams(
            collective_id=0, has_side_effects=True, vmem_limit_bytes=64 * 2**20
        ),
        name="step",
    )(
        teacher_in, teacher_fc1, teacher_fc2, tok_in.T, enc_proj.T, codes.reshape(1, ROWS),
        ema_count.reshape(HI, 128), ema_sum, dec_in, head,
    )
    final = [(HI, 128), (CD, 8192), (PARTS, GROW, 256), (CD, 768), (CD, 192)]
    outs = pl.pallas_call(
        results,
        out_shape=tuple(jax.ShapeDtypeStruct(shape, F32) for shape in final),
        in_specs=[pl.BlockSpec(memory_space=pltpu.HBM)] * 4,
        out_specs=(pl.BlockSpec(memory_space=pltpu.HBM),) * 5,
        scratch_shapes=[vm(final[0], F32), vm(final[1], F32)]
        + [vm((PARTS, GROW, 256), BF16), vm((PARTS, XROW, 128), BF16)]
        + [vm(shape, F32) for shape in final[2:]]
        + [sems(10), sems(11)],
        compiler_params=pltpu.CompilerParams(vmem_limit_bytes=64 * 2**20),
        name="results",
    )(*outs)
    return (outs[0].reshape(8192), outs[1], outs[2].reshape(768, 256), outs[3], outs[4].T)


def solution(mesh):
    placed = (
        P("dp", None),
        P(None, "mp"),
        P("mp", None),
        P("dp", "mp"),
        P("mp", None),
        P("dp"),
        P(),
        P(),
        P(),
        P(None, "mp"),
    )
    return jax.shard_map(
        on_device,
        mesh=mesh,
        in_specs=placed,
        out_specs=(P(), P(), P(None, "mp"), P(), P("mp", None)),
        check_vma=False,
    )
```
